512 devices in a mesh: row: 32 (over y, x, z_hi), col: 16 (over z_lo, core).
Axes of the slice: x: 4, y: 4, z: 16 (z_hi: 2, z_lo: 8; z = z_hi * 8 + z_lo), core: 2. Of those that a mesh axis runs over, the one named last changes fastest.
Arguments:
- kernel_tiles: float32 [32, 16, 32, 128, 128], P('row', 'col'), may hold values from -0.0234375 to 0.0234375
- basis: float32 [64, 32, 16, 128], P(None, 'row', 'col'), may hold values from -6 to 6
Outputs:
- orthobasis: float32 [64, 32, 16, 128], P(None, 'row', 'col')
- cholesky_factor: float32 [64, 64], replicated
The draws below stay inside these ranges and needn't reach their ends.
All inputs are finite; a program needn't handle non-finite values.
Results may differ from the reference program's by a relative error of at most 0.0003.
Values sent between devices are 32-bit elements; how exact they have to be, the bound alone decides.
A program may use at most 64 MiB of HBM per device.

```python
import jax
import jax.numpy as jnp
from jax import lax

SUB = 64
TILE = 128
CT_DEV = 32
ITERS = 2
N = 65536
N_ROW = 32
N_COL = 16


def block_levels(own_key, shape, split, smallest, largest):
    def one(axis_at, blocks):
        heights = jax.random.uniform(jax.random.fold_in(jax.random.fold_in(own_key, 6), axis_at), (blocks,), jnp.float32, smallest / len(split), largest / len(split))
        return jnp.repeat(jnp.exp(heights), shape[axis_at] // blocks).reshape((-1,) + (1,) * (len(shape) - axis_at - 1))

    level = one(*split[0])
    for cut in split[1:]:
        level = level * one(*cut)
    return level


def bell_draw(key, extent, spread, bound, cuts=(), kind=jnp.bfloat16):
    drawn = jax.random.normal(key, extent, jnp.float32) * spread
    if len(cuts) > 0:
        drawn = block_levels(key, extent, cuts, -0.22, 0.18) * drawn
    return jnp.clip(drawn, min=-bound, max=bound).astype(kind)


def setup_inputs(seed: int = 0) -> dict:
    arg_keys = jax.random.split(jax.random.key(seed), 3)
    kernel_tiles = bell_draw(arg_keys[0], (N_ROW, N_COL, CT_DEV, TILE, TILE), N ** -0.5, 0.0234375, ((0, 32), (1, 16)), jnp.float32)
    basis = bell_draw(arg_keys[1], (SUB, CT_DEV, N_COL, TILE), 1.0, 6.0, ((1, 32), (2, 16)), jnp.float32)
    return dict(kernel_tiles=kernel_tiles, basis=basis)


def reference(kernel_tiles, basis):
    tile_total = CT_DEV * N_COL
    order_total = tile_total * TILE
    column_ids = jnp.arange(tile_total, dtype=jnp.int32)
    highest = lax.Precision.HIGHEST
    factor = basis.reshape(SUB, order_total)
    cholesky_factor = jnp.zeros((SUB, SUB), jnp.float32)
    for step_index in range(ITERS):
        factor_tiles = factor.reshape(SUB, tile_total, TILE)

        def advance(carried, inputs):
            stored, tile_row = inputs
            row_tiles = jnp.transpose(stored, (1, 0, 2, 3)).reshape(tile_total, TILE, TILE)
            upper_mask = (column_ids > tile_row).astype(jnp.float32)
            own_tile = lax.dynamic_index_in_dim(factor_tiles, tile_row, 1, keepdims=False)
            direct = jnp.einsum('jts,kjs->kt', row_tiles, factor_tiles * upper_mask[None, :, None], precision=highest)
            diag_tile = lax.dynamic_index_in_dim(row_tiles, tile_row, 0, keepdims=False)
            direct = direct + jnp.einsum('ts,ks->kt', 0.5 * (diag_tile + diag_tile.T), own_tile, precision=highest)
            transposed = jnp.einsum('jts,kt->kjs', row_tiles, own_tile, precision=highest) * upper_mask[None, :, None]
            return (carried + transposed, direct)
        start_sum = jnp.zeros((SUB, tile_total, TILE), jnp.float32)
        product, directs = lax.scan(advance, start_sum, (kernel_tiles, jnp.arange(N_ROW, dtype=jnp.int32)))
        product = product.at[:, :N_ROW, :].add(jnp.transpose(directs, (1, 0, 2)))
        gram_sum = jnp.einsum('kjt,ljt->kl', product, product, precision=highest) / order_total
        cholesky_factor = jnp.linalg.cholesky(gram_sum)
        factor = jax.scipy.linalg.solve_triangular(cholesky_factor, product.reshape(SUB, order_total), lower=True)
    return (factor.reshape(SUB, CT_DEV, N_COL, TILE), cholesky_factor)
```

```python
import functools

import jax
import jax.numpy as jnp
from jax import lax
from jax.experimental import pallas as pl
from jax.experimental.pallas import tpu as pltpu
from jax.sharding import PartitionSpec as P

MESH = pl.DeviceIdType.MESH
HI = lax.Precision.HIGHEST
F32 = jnp.float32
BF16 = jnp.bfloat16


def split(x):
    hi = x.astype(BF16)
    return hi, (x - hi.astype(F32)).astype(BF16)


def nt(a, b):
    return lax.dot_general(a, b, (((1,), (1,)), ((), ())), preferred_element_type=F32)


def nt_high(a, b):
    return lax.dot_general(
        a, b, (((1,), (1,)), ((), ())), precision=HI, preferred_element_type=F32
    )


def factorize(gram):
    n = gram.shape[0]
    eye = (
        lax.broadcasted_iota(jnp.int32, (n, n), 0) == lax.broadcasted_iota(jnp.int32, (n, n), 1)
    ).astype(F32)
    full = jnp.concatenate([gram, eye], axis=1)
    blocks = [full[8 * j : 8 * j + 8] for j in range(n // 8)]
    below = lax.broadcasted_iota(jnp.int32, (8, 1), 0)
    for k in range(n):
        at, sub = divmod(k, 8)
        row = blocks[at][sub : sub + 1]
        pivot = row[:, k : k + 1]
        scaled = row * (1.0 / pivot)
        for j in range(at, n // 8):
            column = blocks[j][:, k : k + 1]
            if j == at:
                column = jnp.where(below > sub, column, 0.0)
            blocks[j] = blocks[j] - column * scaled
    full = jnp.concatenate(blocks, axis=0)
    diagonal = jnp.sum(full[:, :n] * eye, axis=1, keepdims=True)
    return full * lax.rsqrt(diagonal)


def kernel(nrow, ncol, k_ref, v_ref, out_ref, chol_ref, *scratch):
    (
        kh, kl, vc, ktr, vg0, vg1, ps1, ps2, pr1, pr2, zs1, zr1, zs2, zr2, troot,
        ds1, dr1, ds2, dr2, tp0, tg0, tg1, hs, hp, hz,
        gs, gr, gp, gz, gq, ga,
        kq, tps, z_sem, ag_sem, rs_sem, col_sem, top_sem, hz_sem, g_sem,
        s_one, s_xy, s_rs, s_col, s_top, s_g, s_h,
    ) = scratch
    nxy = nrow // 2
    nline = 2 * ncol
    band = nrow // ncol
    row, col = lax.axis_index("row"), lax.axis_index("col")
    xy, zh = row // 2, row % 2
    other = 1 - zh
    sub, tile = v_ref.shape
    order = nrow * ncol * tile
    member = zh * ncol + col
    home = row // ncol
    is_root = col == row % ncol
    holds = row < band
    self_held = jnp.logical_and(row == home, is_root)
    zpart = (xy * 2 + other, col)

    def plane(k):
        return (lax.rem(xy + k, nxy) * 2 + zh, col)

    def in_col(k):
        return (row, lax.rem(col + k, ncol))

    def in_line(k):
        at = lax.rem(member + k, nline)
        return (xy * 2 + at // ncol, lax.rem(at, ncol))

    def mirror(b):
        return (b * ncol + col, lax.rem(row, ncol))

    def holder():
        return (home, lax.rem(row, ncol))

    def held_member(p):
        return (row * ncol + col, p)

    def each(n, body, start=1):
        def step(k, carry):
            body(k)
            return carry

        lax.fori_loop(start, n, step, 0)

    def push(src, dst, s, r, where):
        pltpu.make_async_remote_copy(
            src_ref=src, dst_ref=dst, send_sem=s, recv_sem=r, device_id=where, device_id_type=MESH
        ).start()

    def take(ref, sem):
        pltpu.make_async_copy(ref, ref, sem).wait()

    bar = pltpu.get_barrier_semaphore()

    def greet(where):
        pl.semaphore_signal(bar, inc=1, device_id=where, device_id_type=MESH)

    each(nxy, lambda k: greet(plane(k)))
    each(nline, lambda k: greet(in_line(k)))
    for b in range(band):
        pl.when(b * ncol + col != row)(functools.partial(lambda b: greet(mirror(b)), b))
    pl.when(jnp.logical_not(self_held))(lambda: greet(holder()))

    @pl.when(holds)
    def _():
        def one(p):
            same = jnp.logical_and(row * ncol + col == row, p == col)
            pl.when(jnp.logical_not(same))(lambda: greet(held_member(p)))

        each(ncol, one, 0)

    def cut(q):
        for zd in range(2):
            hi, lo = split(k_ref[2 * q + zd])
            kh[zd, :, q * tile : (q + 1) * tile] = hi
            kl[zd, :, q * tile : (q + 1) * tile] = lo

    for q in range(1, nxy):
        cut(q)
    tile0 = v_ref[...]
    vg0[zh, xy] = tile0

    @pl.when(holds)
    def _():
        spread = jnp.concatenate([tile0, tile0], axis=0).T
        hs[...] = spread.reshape(hs.shape)

    greeted = (nxy - 1) + (nline - 1) + band - is_root.astype(jnp.int32)
    greeted = greeted + jnp.where(self_held, 0, 1)
    greeted = greeted + jnp.where(holds, ncol, 0) - jnp.where(self_held, 1, 0)
    pl.semaphore_wait(bar, greeted)

    push(v_ref, vg0.at[zh, xy], s_one.at[0], z_sem.at[0], zpart)

    @pl.when(holds)
    def _():
        def one(p):
            same = jnp.logical_and(row * ncol + col == row, p == col)
            pl.when(jnp.logical_not(same))(
                lambda: push(hs.at[p], tp0, s_h.at[0], tps.at[0], held_member(p))
            )

        each(ncol, one, 0)

    each(nxy, lambda k: push(v_ref, vg0.at[zh, xy], s_xy.at[0], ag_sem.at[0, 0], plane(k)))
    for b in range(band):

        @pl.when(row < b * ncol + col)
        def _(b=b):
            push(k_ref.at[b], ktr.at[home], s_one.at[4 + b], kq.at[home], mirror(b))

    def all_in_col(src, dst, n):
        each(ncol, lambda k: push(src, dst, s_col.at[n], col_sem.at[n], in_col(k)))

    @pl.when(self_held)
    def _():
        tp0[...] = hs[col]

    @pl.when(jnp.logical_not(self_held))
    def _():
        take(tp0, tps.at[0])

    tg0[col] = tp0[...]
    all_in_col(tp0, tg0.at[col], 0)

    take(vg0.at[other, xy], z_sem.at[0])
    each(
        nxy,
        lambda k: push(
            vg0.at[other, xy], vg0.at[other, xy], s_xy.at[1], ag_sem.at[0, 1], plane(k)
        ),
    )

    def upright(pieces):
        return pieces[...].reshape(tile, 2 * sub).T[:sub]

    def spread_products(top, ps, pr, it):
        hi, lo = split(top)
        both = jnp.concatenate([hi, lo], axis=0)
        for turn in range(2):
            zd = other if turn == 0 else zh
            wide = jnp.dot(both, kh[zd, :, tile:], preferred_element_type=F32)
            wide = wide[:sub] + wide[sub:]
            wide = wide + jnp.dot(hi, kl[zd, :, tile:], preferred_element_type=F32)
            for q in range(1, nxy):
                ps[zd, q] = wide[:, (q - 1) * tile : q * tile]

            def one(k):
                q = lax.rem(xy + k, nxy)
                pl.when(q != 0)(
                    lambda: push(
                        ps.at[zd, q], pr.at[zd, xy], s_rs.at[it, turn], rs_sem.at[it, turn], plane(k)
                    )
                )

            each(nxy, one)

    take(tg0.at[pl.ds(0, ncol - 1)], col_sem.at[0])
    spread_products(upright(tg0), ps1, pr1, 0)

    def lay(vg, zd, q):
        hi, lo = split(vg[zd, q])
        vc[zd, :sub, q * tile : (q + 1) * tile] = hi
        vc[zd, sub:, q * tile : (q + 1) * tile] = lo

    def direct(first, last):
        cols = slice(first * tile, last * tile)
        total = jnp.zeros((tile, 2 * sub), F32)
        for zd in range(2):
            total = total + nt(kh[zd, :, cols], vc[zd, :, cols])
            total = total + nt(kl[zd, :, cols], vc[zd, :, cols])
        return total

    def scatter_direct(total, ds, dr, n):
        total = total + pltpu.roll(total, sub, 1)
        ds[...] = total.reshape(ds.shape)
        dr[col] = ds[col]

        def one(k):
            at = lax.rem(col + k, ncol)
            push(ds.at[at], dr.at[col], s_col.at[n], col_sem.at[n], in_col(k))

        each(ncol, one)

    for b in range(band):

        @pl.when(row < b * ncol + col)
        def _(b=b):
            ktr[b] = k_ref[b]

        @pl.when(row == b * ncol + col)
        def _(b=b):
            ktr[b] = 0.5 * (k_ref[b] + k_ref[b].T)

        @pl.when(row > b * ncol + col)
        def _(b=b):
            take(ktr.at[b], kq.at[b])
            ktr[b] = ktr[b].T

        hi, lo = split(ktr[b])
        kh[b, :, :tile] = hi
        kl[b, :, :tile] = lo

    take(vg0.at[0, pl.ds(0, nxy - 1)], ag_sem.at[0, 0])
    take(vg0.at[0, pl.ds(0, nxy - 1)], ag_sem.at[0, 1])
    for zd in range(2):
        for q in range(nxy):
            lay(vg0, zd, q)
    scatter_direct(direct(0, nxy), ds1, dr1, 1)

    def plane_sum(ps, pr, zd):
        total = ps[zd, xy]
        pr[zd, xy] = total
        total = pr[zd, 0]
        for q in range(1, nxy):
            total = total + pr[zd, q]
        return total

    lower = xy != 0

    def plane_sums(ps, pr, zs, zr, it):
        @pl.when(lower)
        def _():
            take(pr.at[0, pl.ds(0, nxy - 1)], rs_sem.at[it, 0])
            zs[...] = plane_sum(ps, pr, other)
            push(zs, zr, s_one.at[1 + it], z_sem.at[1 + it], zpart)
            take(pr.at[0, pl.ds(0, nxy - 1)], rs_sem.at[it, 1])
            troot[1 + it] = plane_sum(ps, pr, zh)

    plane_sums(ps1, pr1, zs1, zr1, 0)

    def line_sum(ref, count):
        total = ref[0]
        for p in range(1, count):
            total = total + ref[p]
        return total

    take(dr1.at[pl.ds(0, ncol - 1)], col_sem.at[1])
    piece1 = line_sum(dr1, ncol)
    tg1[col] = piece1
    all_in_col(tg1.at[col], tg1.at[col], 2)

    def piece_tile(piece):
        return jnp.concatenate([piece, jnp.zeros((tile - piece.shape[0], tile), F32)], axis=0).T[:sub]

    @pl.when(lower)
    def _():
        take(zr1, z_sem.at[1])
        troot[1] = troot[1] + zr1[...]
        push(troot.at[1], vg1.at[zh, xy], s_one.at[3], z_sem.at[3], zpart)
        each(nxy, lambda k: push(troot.at[1], vg1.at[zh, xy], s_xy.at[2], ag_sem.at[1, 0], plane(k)))
        vg1[zh, xy] = troot[1]

    @pl.when(jnp.logical_not(lower))
    def _():
        troot[1] = jnp.zeros((sub, tile), F32)
        troot[2] = jnp.zeros((sub, tile), F32)

    share = gs.shape[2]

    def gram_out(both, it):
        gram = nt_high(both, both)
        packed = jnp.concatenate([gram[: sub // 2], gram[sub // 2 :]], axis=1)
        for p in range(nxy):
            gs[it, p] = packed[p * share : (p + 1) * share]
        gr[it, xy] = gs[it, xy]

        def one(k):
            q = lax.rem(xy + k, nxy)
            push(gs.at[it, q], gr.at[it, xy], s_g.at[it, 0], g_sem.at[it, 0], plane(k))

        each(nxy, one)

    def gram_line(it):
        take(gr.at[it, pl.ds(0, nxy - 1)], g_sem.at[it, 0])
        gp[it] = line_sum(gr.at[it], nxy)
        gz[it, member] = gp[it]
        each(
            nline,
            lambda k: push(
                gp.at[it], gz.at[it, member], s_g.at[it, 1], g_sem.at[it, 1], in_line(k)
            ),
        )

    def gram_back(it):
        take(gz.at[it, pl.ds(0, nline - 1)], g_sem.at[it, 1])
        gq[it] = line_sum(gz.at[it], nline)
        ga[it, xy] = gq[it]
        each(
            nxy,
            lambda k: push(gq.at[it], ga.at[it, xy], s_g.at[it, 2], g_sem.at[it, 2], plane(k)),
        )

    def gram_in(it):
        take(ga.at[it, pl.ds(0, nxy - 1)], g_sem.at[it, 2])
        packed = jnp.concatenate([ga[it, p] for p in range(nxy)], axis=0)
        gram = jnp.concatenate([packed[:, :sub], packed[:, sub:]], axis=0)
        return gram / order

    gram_out(jnp.concatenate([troot[1], piece_tile(piece1)], axis=1), 0)

    take(tg1.at[pl.ds(0, ncol - 1)], col_sem.at[2])
    top = upright(tg1)

    @pl.when(is_root)
    def _():
        troot[0] = top
        push(troot.at[0], vg1.at[home, 0], s_top.at[1], top_sem.at[home], zpart)
        each(
            nxy,
            lambda k: push(troot.at[0], vg1.at[home, 0], s_top.at[0], top_sem.at[home], plane(k)),
        )
        vg1[home, 0] = top

    spread_products(top, ps2, pr2, 1)

    @pl.when(lower)
    def _():
        take(vg1.at[other, xy], z_sem.at[3])
        each(
            nxy,
            lambda k: push(
                vg1.at[other, xy], vg1.at[other, xy], s_xy.at[3], ag_sem.at[1, 1], plane(k)
            ),
        )

    root_part = col == lax.rem(row + 1 - 2 * zh, ncol)

    @pl.when(root_part)
    def _():
        take(vg1.at[home, 0], top_sem.at[home])
        each(
            nxy,
            lambda k: push(
                vg1.at[home, 0], vg1.at[home, 0], s_top.at[0], top_sem.at[home], plane(k)
            ),
        )

    gram_line(0)

    def take_tiles(ref, sem):
        pl.when(lower)(lambda: take(ref.at[0, pl.ds(0, nxy - 2)], sem))
        pl.when(jnp.logical_not(lower))(lambda: take(ref.at[0, pl.ds(0, nxy - 1)], sem))

    take_tiles(vg1, ag_sem.at[1, 0])
    take_tiles(vg1, ag_sem.at[1, 1])
    for zd in range(2):
        for q in range(1, nxy):
            lay(vg1, zd, q)
    partial = direct(1, nxy)
    for b in range(band):
        mine = jnp.logical_and(home == b, jnp.logical_or(is_root, root_part))
        pl.when(jnp.logical_not(mine))(functools.partial(lambda b: take(vg1.at[b, 0], top_sem.at[b]), b))
        lay(vg1, b, 0)
    scatter_direct(partial + direct(0, 1), ds2, dr2, 3)

    gram_back(0)
    plane_sums(ps2, pr2, zs2, zr2, 1)
    first = factorize(gram_in(0))
    back = first[:, sub:]

    take(dr2.at[pl.ds(0, ncol - 1)], col_sem.at[3])
    hp[...] = line_sum(dr2, ncol)

    @pl.when(self_held)
    def _():
        hz[col] = hp[...]

    @pl.when(jnp.logical_not(self_held))
    def _():
        push(hp, hz.at[col], s_h.at[1], hz_sem.at[0], holder())

    @pl.when(lower)
    def _():
        take(zr2, z_sem.at[2])
        troot[2] = troot[2] + zr2[...]

    both = jnp.concatenate([troot[2], piece_tile(hp[...])], axis=1)
    both = jnp.dot(back, both, precision=HI, preferred_element_type=F32)
    gram_out(both, 1)
    troot[3] = both[:, :tile]
    gram_line(1)

    @pl.when(holds)
    def _():
        pl.when(self_held)(lambda: take(hz.at[pl.ds(0, ncol - 1)], hz_sem.at[0]))
        pl.when(jnp.logical_not(self_held))(lambda: take(hz, hz_sem.at[0]))
        troot[3] = jnp.dot(back, upright(hz), precision=HI, preferred_element_type=F32)

    gram_back(1)
    second = factorize(gram_in(1))
    out_ref[...] = jnp.dot(second[:, sub:], troot[3], precision=HI, preferred_element_type=F32)
    keep = lax.broadcasted_iota(jnp.int32, (sub, sub), 0) >= lax.broadcasted_iota(
        jnp.int32, (sub, sub), 1
    )
    square = jnp.concatenate([second, second], axis=0).T[:sub, :sub]
    chol_ref[...] = jnp.where(keep, square, 0.0)

    many = nxy - 1
    take(v_ref, s_one.at[0])
    take(vg0.at[0, pl.ds(0, many)], s_xy.at[0])
    take(vg0.at[0, pl.ds(0, many)], s_xy.at[1])
    for b in range(band):
        pl.when(row < b * ncol + col)(
            functools.partial(lambda b: take(k_ref.at[b], s_one.at[4 + b]), b)
        )

    @pl.when(holds)
    def _():
        pl.when(self_held)(lambda: take(hs.at[pl.ds(0, ncol - 1)], s_h.at[0]))
        pl.when(jnp.logical_not(self_held))(lambda: take(hs, s_h.at[0]))

    pl.when(jnp.logical_not(self_held))(lambda: take(hp, s_h.at[1]))
    for n in range(4):
        take(tg0.at[pl.ds(0, ncol - 1)], s_col.at[n])
    for it in range(2):
        for turn in range(2):
            pl.when(lower)(lambda: take(pr1.at[0, pl.ds(0, many - 1)], s_rs.at[it, turn]))
            pl.when(jnp.logical_not(lower))(lambda: take(pr1.at[0, pl.ds(0, many)], s_rs.at[it, turn]))
        take(gs.at[it, pl.ds(0, many)], s_g.at[it, 0])
        take(gz.at[it, pl.ds(0, nline - 1)], s_g.at[it, 1])
        take(gs.at[it, pl.ds(0, many)], s_g.at[it, 2])

    @pl.when(lower)
    def _():
        take(zs1, s_one.at[1])
        take(zs2, s_one.at[2])
        take(zs1, s_one.at[3])
        take(vg1.at[0, pl.ds(0, many)], s_xy.at[2])
        take(vg1.at[0, pl.ds(0, many)], s_xy.at[3])

    @pl.when(is_root)
    def _():
        take(zs1, s_top.at[1])
        take(vg1.at[0, pl.ds(0, many)], s_top.at[0])

    @pl.when(root_part)
    def _():
        take(vg1.at[0, pl.ds(0, many)], s_top.at[0])


def per_device(nrow, ncol, kernel_tiles, basis):
    tiles, tile = kernel_tiles.shape[2], kernel_tiles.shape[3]
    sub = basis.shape[0]
    nxy, band, nline = nrow // 2, nrow // ncol, 2 * ncol
    planes = (2, nxy, sub, tile)
    pieces = (ncol, tile // ncol, 2 * sub)
    share = sub // 2 // nxy
    wide = 2 * sub
    vmem = lambda shape, kind=F32: pltpu.VMEM(shape, kind)
    dma = lambda *shape: pltpu.SemaphoreType.DMA(shape)
    scratch = [
        vmem((2, tile, nxy * tile), BF16), vmem((2, tile, nxy * tile), BF16),
        vmem((2, 2 * sub, nxy * tile), BF16), vmem((band, tile, tile)),
        vmem(planes), vmem(planes), vmem(planes), vmem(planes), vmem(planes), vmem(planes),
        vmem((sub, tile)), vmem((sub, tile)), vmem((sub, tile)), vmem((sub, tile)),
        vmem((4, sub, tile)),
        vmem(pieces), vmem(pieces), vmem(pieces), vmem(pieces),
        vmem(pieces[1:]), vmem(pieces), vmem(pieces), vmem(pieces), vmem(pieces[1:]), vmem(pieces),
        vmem((2, nxy, share, wide)), vmem((2, nxy, share, wide)), vmem((2, share, wide)),
        vmem((2, nline, share, wide)), vmem((2, share, wide)), vmem((2, nxy, share, wide)),
        dma(band), dma(1), dma(4), dma(2, 2), dma(2, 2), dma(4), dma(band), dma(1), dma(2, 3),
        dma(4 + band), dma(4), dma(2, 2), dma(4), dma(2), dma(2, 3), dma(2),
    ]
    flops = 2 * 3 * 4 * tiles * tile * tile * sub
    out, chol = pl.pallas_call(
        functools.partial(kernel, nrow, ncol),
        out_shape=(
            jax.ShapeDtypeStruct((sub, tile), F32),
            jax.ShapeDtypeStruct((sub, sub), F32),
        ),
        in_specs=[pl.BlockSpec(memory_space=pltpu.VMEM)] * 2,
        out_specs=(pl.BlockSpec(memory_space=pltpu.VMEM),) * 2,
        scratch_shapes=scratch,
        compiler_params=pltpu.CompilerParams(
            collective_id=0, has_side_effects=True, vmem_limit_bytes=40 * 1024 * 1024
        ),
        cost_estimate=pl.CostEstimate(
            flops=flops, bytes_accessed=4 * tiles * tile * tile, transcendentals=0
        ),
        name="subspace",
    )(kernel_tiles[0, 0], basis.reshape(sub, tile))
    return out.reshape(sub, 1, 1, tile), chol


def solution(mesh):
    nrow, ncol = mesh.shape["row"], mesh.shape["col"]
    return jax.shard_map(
        functools.partial(per_device, nrow, ncol),
        mesh=mesh,
        in_specs=(P("row", "col", None, None, None), P(None, "row", "col", None)),
        out_specs=(P(None, "row", "col", None), P()),
        check_vma=False,
    )
```

```python
import functools

import jax
import jax.numpy as jnp
from jax import lax
from jax.experimental import pallas as pl
from jax.experimental.pallas import tpu as pltpu
from jax.sharding import PartitionSpec as P

MESH = pl.DeviceIdType.MESH
HI = lax.Precision.HIGHEST
F32 = jnp.float32
BF16 = jnp.bfloat16


def split(x):
    hi = x.astype(BF16)
    return hi, (x - hi.astype(F32)).astype(BF16)


def nt(a, b):
    return lax.dot_general(a, b, (((1,), (1,)), ((), ())), preferred_element_type=F32)


def nt_high(a, b):
    return lax.dot_general(
        a, b, (((1,), (1,)), ((), ())), precision=HI, preferred_element_type=F32
    )


def lane(block, k):
    return jnp.broadcast_to(block[:, k : k + 1], (8, block.shape[1]))


def line(block, j):
    return jnp.broadcast_to(block[j : j + 1], (8, block.shape[1]))


def factorize(gram):
    n = gram.shape[0]
    eye = (
        lax.broadcasted_iota(jnp.int32, (n, n), 0) == lax.broadcasted_iota(jnp.int32, (n, n), 1)
    ).astype(F32)
    full = jnp.concatenate([gram, eye], axis=1)
    blocks = [full[8 * j : 8 * j + 8] for j in range(n // 8)]
    at_row = lax.broadcasted_iota(jnp.int32, (8, 2 * n), 0)
    for at in range(n // 8):
        block, first = blocks[at], 8 * at
        columns = [lane(block, first + i) for i in range(8)]
        corner = [[line(columns[i], j) for i in range(j + 1)] for j in range(8)]
        rows = [line(block, j) for j in range(8)]
        inverse = [None] * 8
        ratio = [[None] * 8 for _ in range(8)]
        for i in range(8):
            inverse[i] = 1.0 / corner[i][i]
            for j in range(i + 1, 8):
                ratio[j][i] = corner[j][i] * inverse[i]
            for j in range(i + 1, 8):
                for m in range(i + 1, j + 1):
                    corner[j][m] = corner[j][m] - ratio[j][i] * corner[m][i]
                rows[j] = rows[j] - ratio[j][i] * rows[i]
        scaled = [rows[i] * inverse[i] for i in range(8)]
        for i in range(6, -1, -1):
            for m in range(i + 1, 8):
                scaled[i] = scaled[i] - ratio[m][i] * scaled[m]
        for j in range(at + 1, n // 8):
            terms = [lane(blocks[j], first + i) * scaled[i] for i in range(8)]
            while len(terms) > 1:
                terms = [terms[i] + terms[i + 1] for i in range(0, len(terms), 2)]
            blocks[j] = blocks[j] - terms[0]
        done = rows[0]
        for j in range(1, 8):
            done = jnp.where(at_row == j, rows[j], done)
        blocks[at] = done
    full = jnp.concatenate(blocks, axis=0)
    diagonal = jnp.sum(full[:, :n] * eye, axis=1, keepdims=True)
    return full * lax.rsqrt(diagonal)


def kernel(nrow, ncol, k_ref, v_ref, out_ref, chol_ref, *scratch):
    (
        kv, kh, kl, vc, ktr, vg0, vg1, vtop, ps1, ps2, r1, s2, r2, zs, zr, mine,
        ds1, dr1, ds2, dr2, hs, tp0, tg0, tg1, hp, hz,
        gs, gr, gp, gz, gq, ga,
        ld, kq, tps, z_sem, ag_sem, rs_sem, col_sem, top_sem, hz_sem, g_sem,
        s_one, s_ag, s_rs, s_col, s_top, s_g, s_h,
    ) = scratch
    nxy = nrow // 2
    nline = 2 * ncol
    band = nrow // ncol
    row, col = lax.axis_index("row"), lax.axis_index("col")
    xy, zh = row // 2, row % 2
    side = ps1.shape[1]
    y, x = xy // side, lax.rem(xy, side)
    other = 1 - zh
    sub, tile = v_ref.shape
    order = nrow * ncol * tile
    member = zh * ncol + col
    home = row // ncol
    is_root = col == row % ncol
    holds = row < band
    self_held = jnp.logical_and(row == home, is_root)
    zpart = (xy * 2 + other, col)

    def plane(k):
        return (lax.rem(xy + k, nxy) * 2 + zh, col)

    def along(axis, k):
        if axis == 0:
            return ((lax.rem(y + k, side) * side + x) * 2 + zh, col)
        return ((y * side + lax.rem(x + k, side)) * 2 + zh, col)

    def in_col(k):
        return (row, lax.rem(col + k, ncol))

    def in_line(k):
        at = lax.rem(member + k, nline)
        return (xy * 2 + at // ncol, lax.rem(at, ncol))

    def mirror(b):
        return (b * ncol + col, lax.rem(row, ncol))

    def holder():
        return (home, lax.rem(row, ncol))

    def held_member(p):
        return (row * ncol + col, p)

    def each(n, body, start=1):
        def step(k, carry):
            body(k)
            return carry

        lax.fori_loop(start, n, step, 0)

    def push(src, dst, s, r, where):
        pltpu.make_async_remote_copy(
            src_ref=src, dst_ref=dst, send_sem=s, recv_sem=r, device_id=where, device_id_type=MESH
        ).start()

    def take(ref, sem):
        pltpu.make_async_copy(ref, ref, sem).wait()

    loads = ld.shape[0] - 1
    chunk = nrow // loads

    def load(n):
        part = pl.ds(n * chunk, chunk)
        return pltpu.make_async_copy(k_ref.at[part], kv.at[part], ld.at[n])

    load_v = pltpu.make_async_copy(v_ref, vg0.at[zh, y, x], ld.at[loads])
    load_v.start()
    for n in range(loads):
        load(n).start()

    bar = pltpu.get_barrier_semaphore()

    def greet(where):
        pl.semaphore_signal(bar, inc=1, device_id=where, device_id_type=MESH)

    each(nline, lambda k: greet(in_line(k)))
    each(nxy, lambda k: greet(plane(k)))
    for b in range(band):
        pl.when(b * ncol + col != row)(functools.partial(lambda b: greet(mirror(b)), b))
    pl.when(jnp.logical_not(self_held))(lambda: greet(holder()))

    def held_one(p, act):
        same = jnp.logical_and(row * ncol + col == row, p == col)
        pl.when(jnp.logical_not(same))(act)

    @pl.when(holds)
    def _():
        each(ncol, lambda p: held_one(p, lambda: greet(held_member(p))), 0)

    for zd in range(2):
        ps1[zd, 0, 0] = jnp.zeros((sub, tile), F32)
        ps2[zd, 0, 0] = jnp.zeros((sub, tile), F32)
    for n in range(loads):
        load(n).wait()
        for at in range(max(n * chunk, 2), (n + 1) * chunk):
            q, zd = divmod(at, 2)
            hi, lo = split(kv[at])
            kh[zd, :, q * tile : (q + 1) * tile] = hi
            kl[zd, :, q * tile : (q + 1) * tile] = lo
    load_v.wait()

    @pl.when(holds)
    def _():
        tile0 = vg0[zh, y, x]
        hs[...] = jnp.concatenate([tile0, tile0], axis=0).T.reshape(hs.shape)

    greeted = (nxy - 1) + (nline - 1) + band - is_root.astype(jnp.int32)
    greeted = greeted + jnp.where(self_held, 0, 1)
    greeted = greeted + jnp.where(holds, ncol, 0) - jnp.where(self_held, 1, 0)
    pl.semaphore_wait(bar, greeted)

    @pl.when(holds)
    def _():
        each(
            ncol,
            lambda p: held_one(
                p, lambda: push(hs.at[p], tp0, s_h.at[0], tps.at[0], held_member(p))
            ),
            0,
        )

    push(v_ref, vg0.at[zh, y, x], s_one.at[0], z_sem.at[0], zpart)

    low, high = pl.ds(0, sub // 2), pl.ds(sub // 2, sub // 2)

    def gather_start(src, vg, unit, zd):
        each(
            side,
            lambda k: push(
                src.at[low], vg.at[zd, y, x, low], s_ag.at[unit, 0, 0], ag_sem.at[unit, 0, 0], along(1, k)
            ),
        )
        each(
            side,
            lambda k: push(
                src.at[high], vg.at[zd, y, x, high], s_ag.at[unit, 1, 0], ag_sem.at[unit, 1, 0], along(0, k)
            ),
        )

    def gather_turn(vg, unit, zd):
        take(vg.at[0, 0, pl.ds(0, side - 1), low], ag_sem.at[unit, 0, 0])
        part = vg.at[zd, y, :, low]
        each(side, lambda k: push(part, part, s_ag.at[unit, 0, 1], ag_sem.at[unit, 0, 1], along(0, k)))
        take(vg.at[0, 0, pl.ds(0, side - 1), low], ag_sem.at[unit, 1, 0])
        rest = vg.at[zd, :, x, high]
        each(side, lambda k: push(rest, rest, s_ag.at[unit, 1, 1], ag_sem.at[unit, 1, 1], along(1, k)))

    def gather_end(vg, unit):
        take(vg.at[0, pl.ds(0, side - 1), :, low], ag_sem.at[unit, 0, 1])
        take(vg.at[0, pl.ds(0, side - 1), :, low], ag_sem.at[unit, 1, 1])

    gather_start(v_ref, vg0, 0, zh)
    for b in range(band):

        @pl.when(row < b * ncol + col)
        def _(b=b):
            push(kv.at[b], ktr.at[home], s_one.at[4 + b], kq.at[home], mirror(b))

    def to_plane(src, dst, s, r):
        each(nxy, lambda k: push(src, dst, s, r, plane(k)))

    def upright(pieces):
        return pieces[...].reshape(tile, 2 * sub).T[:sub]

    def spread_products(top, ps, it, turn):
        hi, lo = top
        zd = other if turn == 0 else zh
        wide = jnp.dot(jnp.concatenate([hi, lo], axis=0), kh[zd, :, tile:], preferred_element_type=F32)
        wide = wide[:sub] + wide[sub:]
        wide = wide + jnp.dot(hi, kl[zd, :, tile:], preferred_element_type=F32)
        for q in range(1, nxy):
            ps[zd, q // side, q % side] = wide[:, (q - 1) * tile : q * tile]
        for half, (axis, rows) in enumerate(((0, low), (1, high))):

            def one(k, half=half, axis=axis, rows=rows):
                at = lax.rem((x if axis else y) + k, side)
                push(
                    ps.at[zd, :, at, rows] if axis else ps.at[zd, at, :, rows],
                    r1.at[it, turn, half, x if axis else y],
                    s_rs.at[it, turn, half, 0],
                    rs_sem.at[it, turn, half, 0],
                    along(axis, k),
                )

            each(side, one)

    def total_of(ref):
        total = ref[0]
        for n in range(1, side):
            total = total + ref[n]
        return total

    def sum_turn(ps, it, turn):
        zd = other if turn == 0 else zh
        for half, (axis, rows) in enumerate(((0, low), (1, high))):
            take(r1.at[0, 0, 0, pl.ds(0, side - 1)], rs_sem.at[it, turn, half, 0])
            r1[it, turn, half, x if axis else y] = ps[zd, :, x, rows] if axis else ps[zd, y, :, rows]
            s2[it, turn, half] = total_of(r1.at[it, turn, half])
            here = y if axis else x
            r2[it, turn, half, here] = s2[it, turn, half, here]

            def one(k, half=half, axis=axis, here=here):
                push(
                    s2.at[it, turn, half, lax.rem(here + k, side)],
                    r2.at[it, turn, half, here],
                    s_rs.at[it, turn, half, 1],
                    rs_sem.at[it, turn, half, 1],
                    along(1 - axis, k),
                )

            each(side, one)

    def sum_end(it, turn):
        halves = []
        for half in range(2):
            take(r2.at[0, 0, 0, pl.ds(0, side - 1)], rs_sem.at[it, turn, half, 1])
            halves.append(total_of(r2.at[it, turn, half]))
        return jnp.concatenate(halves, axis=0)

    def lay(vg, zd, first):
        for q in range(first, nxy):
            hi, lo = split(vg[zd, q // side, q % side])
            vc[zd, :sub, q * tile : (q + 1) * tile] = hi
            vc[zd, sub:, q * tile : (q + 1) * tile] = lo

    def direct(zd, first, last):
        cols = slice(first * tile, last * tile)
        return nt(kh[zd, :, cols], vc[zd, :, cols]) + nt(kl[zd, :, cols], vc[zd, :, cols])

    def scatter_direct(total, ds, dr, n):
        total = total + pltpu.roll(total, sub, 1)
        ds[...] = total.reshape(ds.shape)
        dr[col] = ds[col]

        def one(k):
            at = lax.rem(col + k, ncol)
            push(ds.at[at], dr.at[col], s_col.at[n], col_sem.at[n], in_col(k))

        each(ncol, one)

    def line_sum(ref, count):
        total = ref[0]
        for p in range(1, count):
            total = total + ref[p]
        return total

    def piece_tile(piece):
        return jnp.concatenate([piece, jnp.zeros((tile - piece.shape[0], tile), F32)], axis=0).T[:sub]

    share = gs.shape[2]

    def gram_out(both, it):
        gram = nt_high(both, both)
        packed = jnp.concatenate([gram[: sub // 2], gram[sub // 2 :]], axis=1)
        for p in range(nxy):
            gs[it, p] = packed[p * share : (p + 1) * share]
        gr[it, xy] = gs[it, xy]

        def one(k):
            q = lax.rem(xy + k, nxy)
            push(gs.at[it, q], gr.at[it, xy], s_g.at[it, 0], g_sem.at[it, 0], plane(k))

        each(nxy, one)

    def gram_line(it):
        take(gr.at[it, pl.ds(0, nxy - 1)], g_sem.at[it, 0])
        gp[it] = line_sum(gr.at[it], nxy)
        gz[it, member] = gp[it]
        each(
            nline,
            lambda k: push(
                gp.at[it], gz.at[it, member], s_g.at[it, 1], g_sem.at[it, 1], in_line(k)
            ),
        )

    def gram_back(it):
        take(gz.at[it, pl.ds(0, nline - 1)], g_sem.at[it, 1])
        gq[it] = line_sum(gz.at[it], nline)
        ga[it, xy] = gq[it]
        to_plane(gq.at[it], ga.at[it, xy], s_g.at[it, 2], g_sem.at[it, 2])

    def gram_in(it):
        take(ga.at[it, pl.ds(0, nxy - 1)], g_sem.at[it, 2])
        packed = jnp.concatenate([ga[it, p] for p in range(nxy)], axis=0)
        gram = jnp.concatenate([packed[:, :sub], packed[:, sub:]], axis=0)
        return gram / order

    gather_turn(vg0, 0, zh)

    take(vg0.at[other, y, x], z_sem.at[0])
    gather_start(vg0.at[other, y, x], vg0, 1, other)

    @pl.when(self_held)
    def _():
        tp0[...] = hs[col]

    @pl.when(jnp.logical_not(self_held))
    def _():
        take(tp0, tps.at[0])

    tg0[col] = tp0[...]
    each(ncol, lambda k: push(tp0, tg0.at[col], s_col.at[3], col_sem.at[3], in_col(k)))
    gather_turn(vg0, 1, other)

    for b in range(band):

        @pl.when(row < b * ncol + col)
        def _(b=b):
            ktr[b] = kv[b]

        @pl.when(row == b * ncol + col)
        def _(b=b):
            ktr[b] = 0.5 * (kv[b] + kv[b].T)

        @pl.when(row > b * ncol + col)
        def _(b=b):
            take(ktr.at[b], kq.at[b])
            ktr[b] = ktr[b].T

        hi, lo = split(ktr[b])
        kh[b, :, :tile] = hi
        kl[b, :, :tile] = lo

    gather_end(vg0, 0)
    lay(vg0, zh, 0)
    total = direct(zh, 0, nxy)

    take(tg0.at[pl.ds(0, ncol - 1)], col_sem.at[3])
    top = split(upright(tg0))
    spread_products(top, ps1, 0, 0)

    gather_end(vg0, 1)
    lay(vg0, other, 0)
    scatter_direct(total + direct(other, 0, nxy), ds1, dr1, 0)

    spread_products(top, ps1, 0, 1)
    sum_turn(ps1, 0, 0)

    take(dr1.at[pl.ds(0, ncol - 1)], col_sem.at[0])
    piece1 = line_sum(dr1, ncol)
    tg1[col] = piece1
    each(ncol, lambda k: push(tg1.at[col], tg1.at[col], s_col.at[1], col_sem.at[1], in_col(k)))

    sum_turn(ps1, 0, 1)
    for turn in range(2):
        zs[turn] = sum_end(0, turn)
        push(zs.at[turn], zr.at[turn], s_one.at[1 + turn], z_sem.at[1 + turn], zpart)

    take(tg1.at[pl.ds(0, ncol - 1)], col_sem.at[1])
    top = upright(tg1)

    @pl.when(is_root)
    def _():
        mine[0] = top
        push(mine.at[0], vtop.at[home], s_top.at[1], top_sem.at[home], zpart)
        to_plane(mine.at[0], vtop.at[home], s_top.at[0], top_sem.at[home])
        vtop[home] = top

    parts = split(top)
    spread_products(parts, ps2, 1, 0)

    take(zr.at[0], z_sem.at[1])
    mine[1] = zs[1] + zr[0]
    vg1[zh, y, x] = mine[1]
    gram_out(jnp.concatenate([mine[1], piece_tile(piece1)], axis=1), 0)
    gather_start(mine.at[1], vg1, 2, zh)
    spread_products(parts, ps2, 1, 1)
    take(zr.at[1], z_sem.at[2])
    mine[2] = zs[0] + zr[1]
    vg1[other, y, x] = mine[2]
    gather_start(mine.at[2], vg1, 3, other)

    sum_turn(ps2, 1, 0)
    gather_turn(vg1, 2, zh)
    gram_line(0)
    gather_turn(vg1, 3, other)
    zs[2] = sum_end(1, 0)
    push(zs.at[2], zr.at[2], s_one.at[3], z_sem.at[3], zpart)

    root_part = col == lax.rem(row + 1 - 2 * zh, ncol)

    @pl.when(root_part)
    def _():
        take(vtop.at[home], top_sem.at[home])
        to_plane(vtop.at[home], vtop.at[home], s_top.at[0], top_sem.at[home])

    sum_turn(ps2, 1, 1)
    gather_end(vg1, 2)
    lay(vg1, zh, 1)
    total = direct(zh, 1, nxy)
    gather_end(vg1, 3)
    lay(vg1, other, 1)
    total = total + direct(other, 1, nxy)
    gram_back(0)
    for b in range(band):
        own = jnp.logical_and(home == b, jnp.logical_or(is_root, root_part))
        pl.when(jnp.logical_not(own))(functools.partial(lambda b: take(vtop.at[b], top_sem.at[b]), b))
        hi, lo = split(vtop[b])
        vc[b, :sub, :tile] = hi
        vc[b, sub:, :tile] = lo
        total = total + direct(b, 0, 1)
    scatter_direct(total, ds2, dr2, 2)

    rest = sum_end(1, 1)
    first = factorize(gram_in(0))
    back = first[:, sub:]

    take(dr2.at[pl.ds(0, ncol - 1)], col_sem.at[2])
    hp[...] = line_sum(dr2, ncol)

    @pl.when(self_held)
    def _():
        hz[col] = hp[...]

    @pl.when(jnp.logical_not(self_held))
    def _():
        push(hp, hz.at[col], s_h.at[1], hz_sem.at[0], holder())

    take(zr.at[2], z_sem.at[3])
    both = jnp.concatenate([rest + zr[2], piece_tile(hp[...])], axis=1)
    both = jnp.dot(back, both, precision=HI, preferred_element_type=F32)
    gram_out(both, 1)
    mine[3] = both[:, :tile]
    gram_line(1)

    @pl.when(holds)
    def _():
        pl.when(self_held)(lambda: take(hz.at[pl.ds(0, ncol - 1)], hz_sem.at[0]))
        pl.when(jnp.logical_not(self_held))(lambda: take(hz, hz_sem.at[0]))
        mine[3] = jnp.dot(back, upright(hz), precision=HI, preferred_element_type=F32)

    gram_back(1)
    second = factorize(gram_in(1))
    out_ref[...] = jnp.dot(second[:, sub:], mine[3], precision=HI, preferred_element_type=F32)
    keep = lax.broadcasted_iota(jnp.int32, (sub, sub), 0) >= lax.broadcasted_iota(
        jnp.int32, (sub, sub), 1
    )
    square = jnp.concatenate([second, second], axis=0).T[:sub, :sub]
    chol_ref[...] = jnp.where(keep, square, 0.0)

    many = nxy - 1
    take(mine.at[0], s_one.at[0])
    for n in range(3):
        take(zs.at[n], s_one.at[1 + n])
    for b in range(band):
        pl.when(row < b * ncol + col)(
            functools.partial(lambda b: take(kv.at[b], s_one.at[4 + b]), b)
        )
    for unit in range(4):
        for half in range(2):
            take(vg0.at[0, 0, pl.ds(0, side - 1), low], s_ag.at[unit, half, 0])
            take(vg0.at[0, pl.ds(0, side - 1), :, low], s_ag.at[unit, half, 1])

    @pl.when(holds)
    def _():
        pl.when(self_held)(lambda: take(hs.at[pl.ds(0, ncol - 1)], s_h.at[0]))
        pl.when(jnp.logical_not(self_held))(lambda: take(hs, s_h.at[0]))

    pl.when(jnp.logical_not(self_held))(lambda: take(hp, s_h.at[1]))
    for n in range(4):
        take(tg1.at[pl.ds(0, ncol - 1)], s_col.at[n])
    for it in range(2):
        for turn in range(2):
            for half in range(2):
                take(r1.at[0, 0, 0, pl.ds(0, side - 1)], s_rs.at[it, turn, half, 0])
                take(r2.at[0, 0, 0, pl.ds(0, side - 1)], s_rs.at[it, turn, half, 1])
        take(gs.at[it, pl.ds(0, many)], s_g.at[it, 0])
        take(gz.at[it, pl.ds(0, nline - 1)], s_g.at[it, 1])
        take(gs.at[it, pl.ds(0, many)], s_g.at[it, 2])

    @pl.when(is_root)
    def _():
        take(mine.at[0], s_top.at[1])

    @pl.when(jnp.logical_or(is_root, root_part))
    def _():
        for n in range(side - 1):
            take(vg0.at[0, n], s_top.at[0])
        take(vg0.at[0, 0, pl.ds(0, side - 1)], s_top.at[0])


def per_device(nrow, ncol, kernel_tiles, basis):
    tiles, tile = kernel_tiles.shape[2], kernel_tiles.shape[3]
    sub = basis.shape[0]
    nxy, band, nline = nrow // 2, nrow // ncol, 2 * ncol
    pieces = (ncol, tile // ncol, 2 * sub)
    share = sub // 2 // nxy
    wide = 2 * sub
    vmem = lambda shape, kind=F32: pltpu.VMEM(shape, kind)
    dma = lambda *shape: pltpu.SemaphoreType.DMA(shape)
    side = 4 if nxy == 16 else 2
    halves = (2, 2, 2, side)
    half = (sub // 2, tile)
    planes = (2, side, nxy // side, sub, tile)
    scratch = [
        vmem((tiles, tile, tile)),
        vmem((2, tile, nxy * tile), BF16), vmem((2, tile, nxy * tile), BF16),
        vmem((2, 2 * sub, nxy * tile), BF16), vmem((band, tile, tile)),
        vmem(planes), vmem(planes), vmem((band, sub, tile)), vmem(planes), vmem(planes),
        vmem(halves + (side,) + half), vmem(halves + half), vmem(halves + half),
        vmem((3, sub, tile)), vmem((3, sub, tile)), vmem((4, sub, tile)),
        vmem(pieces), vmem(pieces), vmem(pieces), vmem(pieces),
        vmem(pieces), vmem(pieces[1:]), vmem(pieces), vmem(pieces), vmem(pieces[1:]), vmem(pieces),
        vmem((2, nxy, share, wide)), vmem((2, nxy, share, wide)), vmem((2, share, wide)),
        vmem((2, nline, share, wide)), vmem((2, share, wide)), vmem((2, nxy, share, wide)),
        dma(5), dma(band), dma(1), dma(4), dma(4, 2, 2), dma(2, 2, 2, 2), dma(4), dma(band), dma(1),
        dma(2, 3),
        dma(4 + band), dma(4, 2, 2), dma(2, 2, 2, 2), dma(4), dma(2), dma(2, 3), dma(2),
    ]
    flops = 2 * 3 * 4 * tiles * tile * tile * sub
    out, chol = pl.pallas_call(
        functools.partial(kernel, nrow, ncol),
        out_shape=(
            jax.ShapeDtypeStruct((sub, tile), F32),
            jax.ShapeDtypeStruct((sub, sub), F32),
        ),
        in_specs=[pl.BlockSpec(memory_space=pltpu.HBM)] * 2,
        out_specs=(pl.BlockSpec(memory_space=pltpu.VMEM),) * 2,
        scratch_shapes=scratch,
        compiler_params=pltpu.CompilerParams(
            collective_id=0, has_side_effects=True, vmem_limit_bytes=63 * 1024 * 1024
        ),
        cost_estimate=pl.CostEstimate(
            flops=flops, bytes_accessed=4 * tiles * tile * tile, transcendentals=0
        ),
        name="subspace",
    )(kernel_tiles[0, 0], basis.reshape(sub, tile))
    return out.reshape(sub, 1, 1, tile), chol


def solution(mesh):
    nrow, ncol = mesh.shape["row"], mesh.shape["col"]
    return jax.shard_map(
        functools.partial(per_device, nrow, ncol),
        mesh=mesh,
        in_specs=(P("row", "col", None, None, None), P(None, "row", "col", None)),
        out_specs=(P(None, "row", "col", None), P()),
        check_vma=False,
    )
```

```python
import functools

import jax
import jax.numpy as jnp
from jax import lax
from jax.experimental import pallas as pl
from jax.experimental.pallas import tpu as pltpu
from jax.sharding import PartitionSpec as P

MESH = pl.DeviceIdType.MESH
ORDER = (
    "cut_kernel", "own_turn", "other_start", "top_pieces", "other_turn", "mirrored", "direct_own",
    "spread_other", "direct_other", "spread_own", "turn_other", "direct_sum", "z_other", "turn_own", "z_own",
    "top_tile", "spread_other1", "own_tile", "gram_start", "own_start1", "spread_own1", "other_start1",
    "turn_other1", "own_turn1", "gram_line0", "other_turn1", "z_other1", "top_forward", "turn_own1",
    "gram_back0", "direct_own1", "direct_other1", "direct_top1", "rest_own1", "factor0", "direct_sum1",
)
D_AG = (False, True, False, False)
D_RS = ((True, True), (False, False))
HI = lax.Precision.HIGHEST
F32 = jnp.float32
BF16 = jnp.bfloat16


def split(x):
    hi = x.astype(BF16)
    return hi, (x - hi.astype(F32)).astype(BF16)


def nt(a, b):
    return lax.dot_general(a, b, (((1,), (1,)), ((), ())), preferred_element_type=F32)


def nt_high(a, b):
    return lax.dot_general(
        a, b, (((1,), (1,)), ((), ())), precision=HI, preferred_element_type=F32
    )


def lane(block, k):
    return jnp.broadcast_to(block[:, k : k + 1], (8, block.shape[1]))


def line(block, j):
    return jnp.broadcast_to(block[j : j + 1], (8, block.shape[1]))


def factorize(gram):
    n = gram.shape[0]
    eye = (
        lax.broadcasted_iota(jnp.int32, (n, n), 0) == lax.broadcasted_iota(jnp.int32, (n, n), 1)
    ).astype(F32)
    full = jnp.concatenate([gram, eye], axis=1)
    blocks = [full[8 * j : 8 * j + 8] for j in range(n // 8)]
    at_row = lax.broadcasted_iota(jnp.int32, (8, 2 * n), 0)
    for at in range(n // 8):
        block, first = blocks[at], 8 * at
        columns = [lane(block, first + i) for i in range(8)]
        corner = [[line(columns[i], j) for i in range(j + 1)] for j in range(8)]
        rows = [line(block, j) for j in range(8)]
        inverse = [None] * 8
        ratio = [[None] * 8 for _ in range(8)]
        for i in range(8):
            inverse[i] = 1.0 / corner[i][i]
            for j in range(i + 1, 8):
                ratio[j][i] = corner[j][i] * inverse[i]
            for j in range(i + 1, 8):
                for m in range(i + 1, j + 1):
                    corner[j][m] = corner[j][m] - ratio[j][i] * corner[m][i]
                rows[j] = rows[j] - ratio[j][i] * rows[i]
        scaled = [rows[i] * inverse[i] for i in range(8)]
        for i in range(6, -1, -1):
            for m in range(i + 1, 8):
                scaled[i] = scaled[i] - ratio[m][i] * scaled[m]
        for j in range(at + 1, n // 8):
            terms = [lane(blocks[j], first + i) * scaled[i] for i in range(8)]
            while len(terms) > 1:
                terms = [terms[i] + terms[i + 1] for i in range(0, len(terms), 2)]
            blocks[j] = blocks[j] - terms[0]
        done = rows[0]
        for j in range(1, 8):
            done = jnp.where(at_row == j, rows[j], done)
        blocks[at] = done
    full = jnp.concatenate(blocks, axis=0)
    diagonal = jnp.sum(full[:, :n] * eye, axis=1, keepdims=True)
    return full * lax.rsqrt(diagonal)


def unpacked(packed):
    sub = packed.shape[1] // 2
    return jnp.concatenate([packed[:, :sub], packed[:, sub:]], axis=0)


def finish(order, gram_ref, last_ref, out_ref, chol_ref):
    sub = last_ref.shape[0]
    second = factorize(unpacked(gram_ref[...]) / order)
    out_ref[...] = jnp.dot(second[:, sub:], last_ref[...], precision=HI, preferred_element_type=F32)
    keep = lax.broadcasted_iota(jnp.int32, (sub, sub), 0) >= lax.broadcasted_iota(
        jnp.int32, (sub, sub), 1
    )
    square = jnp.concatenate([second, second], axis=0).T[:sub, :sub]
    chol_ref[...] = jnp.where(keep, square, 0.0)


def kernel(nrow, ncol, k_ref, v_ref, gram_ref, last_ref, *scratch):
    (
        kv, kk, vc, ktr, vg0, vg1, vtop, ps1, ps2, whole, r1, s2, r2, zs, zr, mine,
        ds1, dr1, ds2, dr2, hs, tp0, tg0, tg1, hp, hz,
        gs, gr, gp, gz, gq, ga,
        ld, kq, tps, z_sem, ag_sem, rs_sem, col_sem, top_sem, hz_sem, g_sem,
        s_one, s_ag, s_rs, s_col, s_top, s_g, s_h,
    ) = scratch
    nxy = nrow // 2
    nline = 2 * ncol
    band = nrow // ncol
    row, col = lax.axis_index("row"), lax.axis_index("col")
    xy, zh = row // 2, row % 2
    side = ps1.shape[1]
    y, x = xy // side, lax.rem(xy, side)
    other = 1 - zh
    sub, tile = v_ref.shape
    order = nrow * ncol * tile
    member = zh * ncol + col
    home = row // ncol
    is_root = col == row % ncol
    holds = row < band
    self_held = jnp.logical_and(row == home, is_root)
    zpart = (xy * 2 + other, col)

    def plane(k):
        return (lax.rem(xy + k, nxy) * 2 + zh, col)

    def along(axis, k):
        if axis == 0:
            return ((lax.rem(y + k, side) * side + x) * 2 + zh, col)
        return ((y * side + lax.rem(x + k, side)) * 2 + zh, col)

    def in_col(k):
        return (row, lax.rem(col + k, ncol))

    def in_line(k):
        at = lax.rem(member + k, nline)
        return (xy * 2 + at // ncol, lax.rem(at, ncol))

    def mirror(b):
        return (b * ncol + col, lax.rem(row, ncol))

    def holder():
        return (home, lax.rem(row, ncol))

    def held_member(p):
        return (row * ncol + col, p)

    def each(n, body, start=1):
        def step(k, carry):
            body(k)
            return carry

        if n - start < 4:
            for k in range(start, n):
                body(k)
        else:
            lax.fori_loop(start, n, step, 0)

    def farthest_first(n, body):
        def step(k, carry):
            body(lax.rem(n // 2 + lax.rem(k, 2) * (k + 1) // 2 + (1 - lax.rem(k, 2)) * (n - k // 2), n))
            return carry

        lax.fori_loop(0, n - 1, step, 0)

    def push(src, dst, s, r, where):
        pltpu.make_async_remote_copy(
            src_ref=src, dst_ref=dst, send_sem=s, recv_sem=r, device_id=where, device_id_type=MESH
        ).start()

    def take(ref, sem):
        pltpu.make_async_copy(ref, ref, sem).wait()

    loads = ld.shape[0] - 1
    chunk = nrow // loads

    def load(n):
        part = pl.ds(n * chunk, chunk)
        return pltpu.make_async_copy(k_ref.at[part], kv.at[part], ld.at[n])

    load_v = pltpu.make_async_copy(v_ref, vg0.at[zh, y, x], ld.at[loads])
    load_v.start()
    for n in range(loads):
        load(n).start()

    bar = pltpu.get_barrier_semaphore()

    def greet(where):
        pl.semaphore_signal(bar, inc=1, device_id=where, device_id_type=MESH)

    each(nline, lambda k: greet(in_line(k)))
    each(nxy, lambda k: greet(plane(k)))
    for b in range(band):
        pl.when(b * ncol + col != row)(functools.partial(lambda b: greet(mirror(b)), b))
    pl.when(jnp.logical_not(self_held))(lambda: greet(holder()))

    def to_plane(src, dst, s, r):
        each(nxy, lambda k: push(src, dst, s, r, plane(k)))

    def held_one(p, act):
        same = jnp.logical_and(row * ncol + col == row, p == col)
        pl.when(jnp.logical_not(same))(act)

    @pl.when(holds)
    def _():
        each(ncol, lambda p: held_one(p, lambda: greet(held_member(p))), 0)

    load_v.wait()

    @pl.when(holds)
    def _():
        tile0 = vg0[zh, y, x]
        hs[...] = jnp.concatenate([tile0, tile0], axis=0).T.reshape(hs.shape)

    greeted = (nxy - 1) + (nline - 1) + band - is_root.astype(jnp.int32)
    greeted = greeted + jnp.where(self_held, 0, 1)
    greeted = greeted + jnp.where(holds, ncol, 0) - jnp.where(self_held, 1, 0)
    pl.semaphore_wait(bar, greeted)

    @pl.when(holds)
    def _():
        each(
            ncol,
            lambda p: held_one(
                p, lambda: push(hs.at[p], tp0, s_h.at[0], tps.at[0], held_member(p))
            ),
            0,
        )

    push(v_ref, vg0.at[zh, y, x], s_one.at[0], z_sem.at[0], zpart)

    low, high = pl.ds(0, sub // 2), pl.ds(sub // 2, sub // 2)

    def gather_start(src, vg, unit, zd):
        if D_AG[unit]:
            to_plane(src, vg.at[zd, y, x], s_ag.at[unit, 0, 0], ag_sem.at[unit, 0, 0])
            return
        each(
            side,
            lambda k: push(
                src.at[low], vg.at[zd, y, x, low], s_ag.at[unit, 0, 0], ag_sem.at[unit, 0, 0], along(1, k)
            ),
        )
        each(
            side,
            lambda k: push(
                src.at[high], vg.at[zd, y, x, high], s_ag.at[unit, 1, 0], ag_sem.at[unit, 1, 0], along(0, k)
            ),
        )

    def gather_turn(vg, unit, zd):
        if D_AG[unit]:
            return
        take(vg.at[0, 0, pl.ds(0, side - 1), low], ag_sem.at[unit, 0, 0])
        part = vg.at[zd, y, :, low]
        each(side, lambda k: push(part, part, s_ag.at[unit, 0, 1], ag_sem.at[unit, 0, 1], along(0, k)))
        take(vg.at[0, 0, pl.ds(0, side - 1), low], ag_sem.at[unit, 1, 0])
        rest = vg.at[zd, :, x, high]
        each(side, lambda k: push(rest, rest, s_ag.at[unit, 1, 1], ag_sem.at[unit, 1, 1], along(1, k)))

    def gather_end(vg, unit):
        if D_AG[unit]:
            take(whole.at[0, 0, pl.ds(0, nxy - 1)], ag_sem.at[unit, 0, 0])
            return
        take(vg.at[0, pl.ds(0, side - 1), :, low], ag_sem.at[unit, 0, 1])
        take(vg.at[0, pl.ds(0, side - 1), :, low], ag_sem.at[unit, 1, 1])

    gather_start(v_ref, vg0, 0, zh)
    for b in range(band):

        @pl.when(row < b * ncol + col)
        def _(b=b):
            push(k_ref.at[b], ktr.at[home], s_one.at[4 + b], kq.at[home], mirror(b))

    def upright(pieces):
        return pieces[...].reshape(tile, 2 * sub).T[:sub]

    def paired(top):
        hi, lo = split(top)
        return jnp.concatenate(
            [jnp.concatenate([hi, hi], axis=1), jnp.concatenate([lo, jnp.zeros_like(lo)], axis=1)], axis=0
        )

    def spread_products(top, ps, it, turn):
        zd = other if turn == 0 else zh
        wide = jnp.dot(top, kk[zd, :, tile:], preferred_element_type=F32)
        wide = wide[:sub] + wide[sub:]
        for q in range(1, nxy):
            ps[zd, q // side, q % side] = wide[:, (q - 1) * tile : q * tile]
        if D_RS[it][turn]:

            def whole_one(k):
                at = lax.rem(xy + k, nxy)
                push(
                    ps.at[zd, at // side, lax.rem(at, side)],
                    whole.at[it, turn, xy],
                    s_rs.at[it, turn, 0, 0],
                    rs_sem.at[it, turn, 0, 0],
                    plane(k),
                )

            each(nxy, whole_one)
            return
        for half, (axis, rows) in enumerate(((0, low), (1, high))):

            def one(k, half=half, axis=axis, rows=rows):
                at = lax.rem((x if axis else y) + k, side)
                push(
                    ps.at[zd, :, at, rows] if axis else ps.at[zd, at, :, rows],
                    r1.at[it, turn, half, x if axis else y],
                    s_rs.at[it, turn, half, 0],
                    rs_sem.at[it, turn, half, 0],
                    along(axis, k),
                )

            each(side, one)

    def total_of(ref):
        total = ref[0]
        for n in range(1, side):
            total = total + ref[n]
        return total

    def sum_turn(ps, it, turn):
        if D_RS[it][turn]:
            return
        zd = other if turn == 0 else zh
        for half, (axis, rows) in enumerate(((0, low), (1, high))):
            take(r1.at[0, 0, 0, pl.ds(0, side - 1)], rs_sem.at[it, turn, half, 0])
            r1[it, turn, half, x if axis else y] = ps[zd, :, x, rows] if axis else ps[zd, y, :, rows]
            s2[it, turn, half] = total_of(r1.at[it, turn, half])
            here = y if axis else x
            r2[it, turn, half, here] = s2[it, turn, half, here]

            def one(k, half=half, axis=axis, here=here):
                push(
                    s2.at[it, turn, half, lax.rem(here + k, side)],
                    r2.at[it, turn, half, here],
                    s_rs.at[it, turn, half, 1],
                    rs_sem.at[it, turn, half, 1],
                    along(1 - axis, k),
                )

            each(side, one)

    def sum_end(ps, it, turn):
        if D_RS[it][turn]:
            take(whole.at[0, 0, pl.ds(0, nxy - 1)], rs_sem.at[it, turn, 0, 0])
            whole[it, turn, xy] = ps[other if turn == 0 else zh, y, x]
            total = whole[it, turn, 0]
            for n in range(1, nxy):
                total = total + whole[it, turn, n]
            return total
        halves = []
        for half in range(2):
            take(r2.at[0, 0, 0, pl.ds(0, side - 1)], rs_sem.at[it, turn, half, 1])
            halves.append(total_of(r2.at[it, turn, half]))
        return jnp.concatenate(halves, axis=0)

    def lay(vg, zd, first):
        for q in range(first, nxy):
            hi, lo = split(vg[zd, q // side, q % side])
            vc[zd, :sub, q * tile : (q + 1) * tile] = hi
            vc[zd, sub:, q * tile : (q + 1) * tile] = lo

    def direct(zd, first, last):
        cols = slice(first * tile, last * tile)
        both = nt(kk[zd, :, cols], vc[zd, :, cols])
        return both[:tile] + both[tile:]

    def scatter_direct(total, ds, dr, n):
        total = total + pltpu.roll(total, sub, 1)
        ds[...] = total.reshape(ds.shape)
        dr[col] = ds[col]

        def one(k):
            at = lax.rem(col + k, ncol)
            push(ds.at[at], dr.at[col], s_col.at[n], col_sem.at[n], in_col(k))

        each(ncol, one)

    def over_z(turn):
        zs[turn] = sum_end(ps1, 0, turn)
        push(zs.at[turn], zr.at[turn], s_one.at[1 + turn], z_sem.at[1 + turn], zpart)

    def line_sum(ref, count):
        total = ref[0]
        for p in range(1, count):
            total = total + ref[p]
        return total

    def piece_tile(piece):
        return jnp.concatenate([piece, jnp.zeros((tile - piece.shape[0], tile), F32)], axis=0).T[:sub]

    share = gs.shape[2]

    def gram_out(both, it):
        gram = nt_high(both, both)
        packed = jnp.concatenate([gram[: sub // 2], gram[sub // 2 :]], axis=1)
        for p in range(nxy):
            gs[it, p] = packed[p * share : (p + 1) * share]
        gr[it, xy] = gs[it, xy]

        def one(k):
            q = lax.rem(xy + k, nxy)
            push(gs.at[it, q], gr.at[it, xy], s_g.at[it, 0], g_sem.at[it, 0], plane(k))

        each(nxy, one)

    def gram_line(it):
        take(gr.at[it, pl.ds(0, nxy - 1)], g_sem.at[it, 0])
        gp[it] = line_sum(gr.at[it], nxy)
        gz[it, member] = gp[it]
        farthest_first(
            nline,
            lambda k: push(
                gp.at[it], gz.at[it, member], s_g.at[it, 1], g_sem.at[it, 1], in_line(k)
            ),
        )

    def gram_back(it):
        take(gz.at[it, pl.ds(0, nline - 1)], g_sem.at[it, 1])
        gq[it] = line_sum(gz.at[it], nline)
        ga[it, xy] = gq[it]
        to_plane(gq.at[it], ga.at[it, xy], s_g.at[it, 2], g_sem.at[it, 2])

    def gram_in(it):
        take(ga.at[it, pl.ds(0, nxy - 1)], g_sem.at[it, 2])
        packed = jnp.concatenate([ga[it, p] for p in range(nxy)], axis=0)
        return unpacked(packed) / order

    kept = {}

    def cut_kernel():
        for zd in range(2):
            ps1[zd, 0, 0] = jnp.zeros((sub, tile), F32)
            ps2[zd, 0, 0] = jnp.zeros((sub, tile), F32)
        for n in range(loads):
            load(n).wait()
            for at in range(max(n * chunk, 2), (n + 1) * chunk):
                q, zd = divmod(at, 2)
                hi, lo = split(kv[at])
                kk[zd, :tile, q * tile : (q + 1) * tile] = hi
                kk[zd, tile:, q * tile : (q + 1) * tile] = lo

    def own_turn():
        gather_turn(vg0, 0, zh)

    def other_start():
        take(vg0.at[other, y, x], z_sem.at[0])
        gather_start(vg0.at[other, y, x], vg0, 1, other)

    def other_turn():
        gather_turn(vg0, 1, other)

    def top_pieces():
        @pl.when(self_held)
        def _():
            tp0[...] = hs[col]

        @pl.when(jnp.logical_not(self_held))
        def _():
            take(tp0, tps.at[0])

        tg0[col] = tp0[...]
        each(ncol, lambda k: push(tp0, tg0.at[col], s_col.at[3], col_sem.at[3], in_col(k)))

    def mirrored():
        for b in range(band):

            @pl.when(row < b * ncol + col)
            def _(b=b):
                ktr[b] = kv[b]

            @pl.when(row == b * ncol + col)
            def _(b=b):
                ktr[b] = 0.5 * (kv[b] + kv[b].T)

            @pl.when(row > b * ncol + col)
            def _(b=b):
                take(ktr.at[b], kq.at[b])
                ktr[b] = ktr[b].T

            hi, lo = split(ktr[b])
            kk[b, :tile, :tile] = hi
            kk[b, tile:, :tile] = lo

    def direct_own():
        gather_end(vg0, 0)
        lay(vg0, zh, 0)
        kept["direct"] = direct(zh, 0, nxy)

    def direct_other():
        gather_end(vg0, 1)
        lay(vg0, other, 0)
        scatter_direct(kept["direct"] + direct(other, 0, nxy), ds1, dr1, 0)

    def spread_other():
        take(tg0.at[pl.ds(0, ncol - 1)], col_sem.at[3])
        kept["top"] = paired(upright(tg0))
        spread_products(kept["top"], ps1, 0, 0)

    def spread_own():
        spread_products(kept["top"], ps1, 0, 1)

    def turn_other():
        sum_turn(ps1, 0, 0)

    def turn_own():
        sum_turn(ps1, 0, 1)

    def z_other():
        over_z(0)

    def z_own():
        over_z(1)

    def direct_sum():
        take(dr1.at[pl.ds(0, ncol - 1)], col_sem.at[0])
        kept["piece"] = line_sum(dr1, ncol)
        tg1[col] = kept["piece"]
        each(ncol, lambda k: push(tg1.at[col], tg1.at[col], s_col.at[1], col_sem.at[1], in_col(k)))

    def top_tile():
        take(tg1.at[pl.ds(0, ncol - 1)], col_sem.at[1])
        top = upright(tg1)
        kept["top1"] = paired(top)

        @pl.when(is_root)
        def _():
            mine[0] = top
            push(mine.at[0], vtop.at[home], s_top.at[1], top_sem.at[home], zpart)
            to_plane(mine.at[0], vtop.at[home], s_top.at[0], top_sem.at[home])
            vtop[home] = top

    def spread_other1():
        spread_products(kept["top1"], ps2, 1, 0)

    def spread_own1():
        spread_products(kept["top1"], ps2, 1, 1)

    def own_tile():
        take(zr.at[0], z_sem.at[1])
        mine[1] = zs[1] + zr[0]
        vg1[zh, y, x] = mine[1]

    def gram_start():
        gram_out(jnp.concatenate([mine[1], piece_tile(kept["piece"])], axis=1), 0)

    def own_start1():
        gather_start(mine.at[1], vg1, 2, zh)

    def other_start1():
        take(zr.at[1], z_sem.at[2])
        mine[2] = zs[0] + zr[1]
        vg1[other, y, x] = mine[2]
        gather_start(mine.at[2], vg1, 3, other)

    def turn_other1():
        sum_turn(ps2, 1, 0)

    def turn_own1():
        sum_turn(ps2, 1, 1)

    def own_turn1():
        gather_turn(vg1, 2, zh)

    def other_turn1():
        gather_turn(vg1, 3, other)

    def gram_line0():
        gram_line(0)

    def gram_back0():
        gram_back(0)

    def z_other1():
        zs[2] = sum_end(ps2, 1, 0)
        push(zs.at[2], zr.at[2], s_one.at[3], z_sem.at[3], zpart)

    root_part = col == lax.rem(row + 1 - 2 * zh, ncol)

    def top_forward():
        @pl.when(root_part)
        def _():
            take(vtop.at[home], top_sem.at[home])
            to_plane(vtop.at[home], vtop.at[home], s_top.at[0], top_sem.at[home])

    def direct_own1():
        gather_end(vg1, 2)
        lay(vg1, zh, 1)
        kept["own1"] = direct(zh, 1, nxy)

    def direct_other1():
        gather_end(vg1, 3)
        lay(vg1, other, 1)
        kept["other1"] = direct(other, 1, nxy)

    def direct_top1():
        total = kept["own1"] + kept["other1"]
        for b in range(band):
            own = jnp.logical_and(home == b, jnp.logical_or(is_root, root_part))
            pl.when(jnp.logical_not(own))(
                functools.partial(lambda b: take(vtop.at[b], top_sem.at[b]), b)
            )
            hi, lo = split(vtop[b])
            vc[b, :sub, :tile] = hi
            vc[b, sub:, :tile] = lo
            total = total + direct(b, 0, 1)
        scatter_direct(total, ds2, dr2, 2)

    def rest_own1():
        kept["rest"] = sum_end(ps2, 1, 1)

    def factor0():
        kept["back"] = factorize(gram_in(0))[:, sub:]

    def direct_sum1():
        take(dr2.at[pl.ds(0, ncol - 1)], col_sem.at[2])
        hp[...] = line_sum(dr2, ncol)

        @pl.when(self_held)
        def _():
            hz[col] = hp[...]

        @pl.when(jnp.logical_not(self_held))
        def _():
            push(hp, hz.at[col], s_h.at[1], hz_sem.at[0], holder())

    steps = dict(
        cut_kernel=cut_kernel, own_turn=own_turn, other_start=other_start, other_turn=other_turn,
        top_pieces=top_pieces, mirrored=mirrored, direct_own=direct_own, direct_other=direct_other,
        spread_other=spread_other, spread_own=spread_own, turn_other=turn_other, turn_own=turn_own,
        z_other=z_other, z_own=z_own, direct_sum=direct_sum, top_tile=top_tile,
        spread_other1=spread_other1, spread_own1=spread_own1, own_tile=own_tile, gram_start=gram_start,
        own_start1=own_start1, other_start1=other_start1, turn_other1=turn_other1, turn_own1=turn_own1,
        own_turn1=own_turn1, other_turn1=other_turn1, gram_line0=gram_line0, gram_back0=gram_back0,
        z_other1=z_other1, top_forward=top_forward, direct_own1=direct_own1, direct_other1=direct_other1,
        direct_top1=direct_top1, rest_own1=rest_own1, factor0=factor0, direct_sum1=direct_sum1,
    )
    for name in ORDER:
        steps[name]()

    back = kept["back"]
    take(zr.at[2], z_sem.at[3])
    both = jnp.concatenate([kept["rest"] + zr[2], piece_tile(hp[...])], axis=1)
    both = jnp.dot(back, both, precision=HI, preferred_element_type=F32)
    gram_out(both, 1)
    mine[3] = both[:, :tile]
    gram_line(1)

    @pl.when(holds)
    def _():
        pl.when(self_held)(lambda: take(hz.at[pl.ds(0, ncol - 1)], hz_sem.at[0]))
        pl.when(jnp.logical_not(self_held))(lambda: take(hz, hz_sem.at[0]))
        mine[3] = jnp.dot(back, upright(hz), precision=HI, preferred_element_type=F32)

    gram_back(1)
    take(ga.at[1, pl.ds(0, nxy - 1)], g_sem.at[1, 2])
    gram_ref[...] = jnp.concatenate([ga[1, p] for p in range(nxy)], axis=0)
    last_ref[...] = mine[3]

    many = nxy - 1
    take(mine.at[0], s_one.at[0])
    for n in range(3):
        take(zs.at[n], s_one.at[1 + n])
    for b in range(band):
        pl.when(row < b * ncol + col)(
            functools.partial(lambda b: take(kv.at[b], s_one.at[4 + b]), b)
        )
    for unit in range(4):
        if D_AG[unit]:
            take(whole.at[0, 0, pl.ds(0, many)], s_ag.at[unit, 0, 0])
            continue
        for half in range(2):
            take(vg0.at[0, 0, pl.ds(0, side - 1), low], s_ag.at[unit, half, 0])
            take(vg0.at[0, pl.ds(0, side - 1), :, low], s_ag.at[unit, half, 1])

    @pl.when(holds)
    def _():
        pl.when(self_held)(lambda: take(hs.at[pl.ds(0, ncol - 1)], s_h.at[0]))
        pl.when(jnp.logical_not(self_held))(lambda: take(hs, s_h.at[0]))

    pl.when(jnp.logical_not(self_held))(lambda: take(hp, s_h.at[1]))
    for n in range(4):
        take(tg1.at[pl.ds(0, ncol - 1)], s_col.at[n])
    for it in range(2):
        for turn in range(2):
            if D_RS[it][turn]:
                take(whole.at[0, 0, pl.ds(0, many)], s_rs.at[it, turn, 0, 0])
                continue
            for half in range(2):
                take(r1.at[0, 0, 0, pl.ds(0, side - 1)], s_rs.at[it, turn, half, 0])
                take(r2.at[0, 0, 0, pl.ds(0, side - 1)], s_rs.at[it, turn, half, 1])
        take(gs.at[it, pl.ds(0, many)], s_g.at[it, 0])
        take(gz.at[it, pl.ds(0, nline - 1)], s_g.at[it, 1])
        take(gs.at[it, pl.ds(0, many)], s_g.at[it, 2])

    @pl.when(is_root)
    def _():
        take(mine.at[0], s_top.at[1])

    @pl.when(jnp.logical_or(is_root, root_part))
    def _():
        take(whole.at[0, 0, pl.ds(0, many)], s_top.at[0])


def per_device(nrow, ncol, kernel_tiles, basis):
    tiles, tile = kernel_tiles.shape[2], kernel_tiles.shape[3]
    sub = basis.shape[0]
    nxy, band, nline = nrow // 2, nrow // ncol, 2 * ncol
    pieces = (ncol, tile // ncol, 2 * sub)
    share = sub // 2 // nxy
    wide = 2 * sub
    vmem = lambda shape, kind=F32: pltpu.VMEM(shape, kind)
    dma = lambda *shape: pltpu.SemaphoreType.DMA(shape)
    side = 4 if nxy == 16 else 2
    halves = (2, 2, 2, side)
    half = (sub // 2, tile)
    planes = (2, side, nxy // side, sub, tile)
    scratch = [
        vmem((tiles, tile, tile)),
        vmem((2, 2 * tile, nxy * tile), BF16),
        vmem((2, 2 * sub, nxy * tile), BF16), vmem((band, tile, tile)),
        vmem(planes), vmem(planes), vmem((band, sub, tile)), vmem(planes), vmem(planes),
        vmem((2, 2, nxy, sub, tile)),
        vmem(halves + (side,) + half), vmem(halves + half), vmem(halves + half),
        vmem((3, sub, tile)), vmem((3, sub, tile)), vmem((4, sub, tile)),
        vmem(pieces), vmem(pieces), vmem(pieces), vmem(pieces),
        vmem(pieces), vmem(pieces[1:]), vmem(pieces), vmem(pieces), vmem(pieces[1:]), vmem(pieces),
        vmem((2, nxy, share, wide)), vmem((2, nxy, share, wide)), vmem((2, share, wide)),
        vmem((2, nline, share, wide)), vmem((2, share, wide)), vmem((2, nxy, share, wide)),
        dma(5), dma(band), dma(1), dma(4), dma(4, 2, 2), dma(2, 2, 2, 2), dma(4), dma(band), dma(1),
        dma(2, 3),
        dma(4 + band), dma(4, 2, 2), dma(2, 2, 2, 2), dma(4), dma(2), dma(2, 3), dma(2),
    ]
    flops = 2 * 3 * 4 * tiles * tile * tile * sub
    gram, last = pl.pallas_call(
        functools.partial(kernel, nrow, ncol),
        out_shape=(
            jax.ShapeDtypeStruct((sub // 2, 2 * sub), F32),
            jax.ShapeDtypeStruct((sub, tile), F32),
        ),
        in_specs=[pl.BlockSpec(memory_space=pltpu.HBM)] * 2,
        out_specs=(pl.BlockSpec(memory_space=pltpu.VMEM),) * 2,
        scratch_shapes=scratch,
        compiler_params=pltpu.CompilerParams(
            collective_id=0, has_side_effects=True, vmem_limit_bytes=63 * 1024 * 1024
        ),
        cost_estimate=pl.CostEstimate(
            flops=flops, bytes_accessed=4 * tiles * tile * tile, transcendentals=0
        ),
        name="subspace",
    )(kernel_tiles[0, 0], basis.reshape(sub, tile))
    out, chol = pl.pallas_call(
        functools.partial(finish, nrow * ncol * tile),
        out_shape=(
            jax.ShapeDtypeStruct((sub, tile), F32),
            jax.ShapeDtypeStruct((sub, sub), F32),
        ),
        in_specs=[pl.BlockSpec(memory_space=pltpu.VMEM)] * 2,
        out_specs=(pl.BlockSpec(memory_space=pltpu.VMEM),) * 2,
        name="finish",
    )(gram, last)
    return out.reshape(sub, 1, 1, tile), chol


def solution(mesh):
    nrow, ncol = mesh.shape["row"], mesh.shape["col"]
    return jax.shard_map(
        functools.partial(per_device, nrow, ncol),
        mesh=mesh,
        in_specs=(P("row", "col", None, None, None), P(None, "row", "col", None)),
        out_specs=(P(None, "row", "col", None), P()),
        check_vma=False,
    )
```

```python
import functools

import jax
import jax.numpy as jnp
from jax import lax
from jax.experimental import pallas as pl
from jax.experimental.pallas import tpu as pltpu
from jax.sharding import PartitionSpec as P

MESH = pl.DeviceIdType.MESH
ORDER = (
    "cut_kernel", "own_turn", "other_start", "top_pieces", "other_turn", "mirrored", "direct_own",
    "direct_other", "spread_other", "spread_own", "turn_other", "direct_sum", "z_other", "turn_own", "z_own",
    "top_tile", "spread_other1", "own_tile", "gram_start", "own_start1", "spread_own1", "other_start1",
    "turn_other1", "own_turn1", "gram_line0", "other_turn1", "z_other1", "top_forward", "turn_own1",
    "gram_back0", "direct_own1", "direct_other1", "direct_top1", "rest_own1", "factor0", "direct_sum1",
)
D_AG = (True, True, False, False)
D_RS = ((True, True), (False, False))
HI = lax.Precision.HIGHEST
F32 = jnp.float32
BF16 = jnp.bfloat16


def split(x):
    hi = x.astype(BF16)
    return hi, (x - hi.astype(F32)).astype(BF16)


def nt(a, b):
    return lax.dot_general(a, b, (((1,), (1,)), ((), ())), preferred_element_type=F32)


def nt_high(a, b):
    return lax.dot_general(
        a, b, (((1,), (1,)), ((), ())), precision=HI, preferred_element_type=F32
    )


def lane(block, k):
    return jnp.broadcast_to(block[:, k : k + 1], (8, block.shape[1]))


def line(block, j):
    return jnp.broadcast_to(block[j : j + 1], (8, block.shape[1]))


def factorize(gram):
    n = gram.shape[0]
    eye = (
        lax.broadcasted_iota(jnp.int32, (n, n), 0) == lax.broadcasted_iota(jnp.int32, (n, n), 1)
    ).astype(F32)
    full = jnp.concatenate([gram, eye], axis=1)
    blocks = [full[8 * j : 8 * j + 8] for j in range(n // 8)]
    at_row = lax.broadcasted_iota(jnp.int32, (8, 2 * n), 0)
    for at in range(n // 8):
        block, first = blocks[at], 8 * at
        columns = [lane(block, first + i) for i in range(8)]
        corner = [[line(columns[i], j) for i in range(j + 1)] for j in range(8)]
        rows = [line(block, j) for j in range(8)]
        inverse = [None] * 8
        ratio = [[None] * 8 for _ in range(8)]
        for i in range(8):
            inverse[i] = 1.0 / corner[i][i]
            for j in range(i + 1, 8):
                ratio[j][i] = corner[j][i] * inverse[i]
            for j in range(i + 1, 8):
                for m in range(i + 1, j + 1):
                    corner[j][m] = corner[j][m] - ratio[j][i] * corner[m][i]
                rows[j] = rows[j] - ratio[j][i] * rows[i]
        scaled = [rows[i] * inverse[i] for i in range(8)]
        for i in range(6, -1, -1):
            for m in range(i + 1, 8):
                scaled[i] = scaled[i] - ratio[m][i] * scaled[m]
        for j in range(at + 1, n // 8):
            terms = [lane(blocks[j], first + i) * scaled[i] for i in range(8)]
            while len(terms) > 1:
                terms = [terms[i] + terms[i + 1] for i in range(0, len(terms), 2)]
            blocks[j] = blocks[j] - terms[0]
        done = rows[0]
        for j in range(1, 8):
            done = jnp.where(at_row == j, rows[j], done)
        blocks[at] = done
    full = jnp.concatenate(blocks, axis=0)
    diagonal = jnp.sum(full[:, :n] * eye, axis=1, keepdims=True)
    return full * lax.rsqrt(diagonal)


def unpacked(packed):
    sub = packed.shape[1] // 2
    return jnp.concatenate([packed[:, :sub], packed[:, sub:]], axis=0)


def finish(order, gram_ref, last_ref, out_ref, chol_ref):
    sub = last_ref.shape[0]
    second = factorize(unpacked(gram_ref[...]) / order)
    out_ref[...] = jnp.dot(second[:, sub:], last_ref[...], precision=HI, preferred_element_type=F32)
    keep = lax.broadcasted_iota(jnp.int32, (sub, sub), 0) >= lax.broadcasted_iota(
        jnp.int32, (sub, sub), 1
    )
    square = jnp.concatenate([second, second], axis=0).T[:sub, :sub]
    chol_ref[...] = jnp.where(keep, square, 0.0)


def kernel(nrow, ncol, k_ref, v_ref, gram_ref, last_ref, *scratch):
    (
        kv, kk, vc, ktr, vg0, vg1, vtop, ps1, ps2, whole, r1, s2, r2, zs, zr, mine,
        ds1, dr1, ds2, dr2, hs, tp0, tg0, tg1, hp, hz,
        gs, gr, gp, gz, gq, ga,
        ld, kq, tps, z_sem, ag_sem, rs_sem, col_sem, top_sem, hz_sem, g_sem,
        s_one, s_ag, s_rs, s_col, s_top, s_g, s_h,
    ) = scratch
    nxy = nrow // 2
    nline = 2 * ncol
    band = nrow // ncol
    row, col = lax.axis_index("row"), lax.axis_index("col")
    xy, zh = row // 2, row % 2
    side = ps1.shape[1]
    y, x = xy // side, lax.rem(xy, side)
    other = 1 - zh
    sub, tile = v_ref.shape
    order = nrow * ncol * tile
    member = zh * ncol + col
    home = row // ncol
    is_root = col == row % ncol
    holds = row < band
    self_held = jnp.logical_and(row == home, is_root)
    zpart = (xy * 2 + other, col)

    def plane(k):
        return (lax.rem(xy + k, nxy) * 2 + zh, col)

    def along(axis, k):
        if axis == 0:
            return ((lax.rem(y + k, side) * side + x) * 2 + zh, col)
        return ((y * side + lax.rem(x + k, side)) * 2 + zh, col)

    def in_col(k):
        return (row, lax.rem(col + k, ncol))

    def in_line(k):
        at = lax.rem(member + k, nline)
        return (xy * 2 + at // ncol, lax.rem(at, ncol))

    def mirror(b):
        return (b * ncol + col, lax.rem(row, ncol))

    def holder():
        return (home, lax.rem(row, ncol))

    def held_member(p):
        return (row * ncol + col, p)

    def each(n, body, start=1):
        def step(k, carry):
            body(k)
            return carry

        if n - start < 4:
            for k in range(start, n):
                body(k)
        else:
            lax.fori_loop(start, n, step, 0)

    def farthest_first(n, body):
        def step(k, carry):
            body(lax.rem(n // 2 + lax.rem(k, 2) * (k + 1) // 2 + (1 - lax.rem(k, 2)) * (n - k // 2), n))
            return carry

        lax.fori_loop(0, n - 1, step, 0)

    def push(src, dst, s, r, where):
        pltpu.make_async_remote_copy(
            src_ref=src, dst_ref=dst, send_sem=s, recv_sem=r, device_id=where, device_id_type=MESH
        ).start()

    def take(ref, sem):
        pltpu.make_async_copy(ref, ref, sem).wait()

    loads = ld.shape[0] - 1
    chunk = nrow // loads

    def load(n):
        part = pl.ds(n * chunk, chunk)
        return pltpu.make_async_copy(k_ref.at[part], kv.at[part], ld.at[n])

    load_v = pltpu.make_async_copy(v_ref, vg0.at[zh, y, x], ld.at[loads])
    load_v.start()
    for n in range(loads):
        load(n).start()

    bar = pltpu.get_barrier_semaphore()

    def greet(where):
        pl.semaphore_signal(bar, inc=1, device_id=where, device_id_type=MESH)

    each(nline, lambda k: greet(in_line(k)))
    each(nxy, lambda k: greet(plane(k)))
    for b in range(band):
        pl.when(b * ncol + col != row)(functools.partial(lambda b: greet(mirror(b)), b))
    pl.when(jnp.logical_not(self_held))(lambda: greet(holder()))

    def to_plane(src, dst, s, r):
        each(nxy, lambda k: push(src, dst, s, r, plane(k)))

    def held_one(p, act):
        same = jnp.logical_and(row * ncol + col == row, p == col)
        pl.when(jnp.logical_not(same))(act)

    @pl.when(holds)
    def _():
        each(ncol, lambda p: held_one(p, lambda: greet(held_member(p))), 0)

    load_v.wait()

    @pl.when(holds)
    def _():
        tile0 = vg0[zh, y, x]
        hs[...] = jnp.concatenate([tile0, tile0], axis=0).T.reshape(hs.shape)

    greeted = (nxy - 1) + (nline - 1) + band - is_root.astype(jnp.int32)
    greeted = greeted + jnp.where(self_held, 0, 1)
    greeted = greeted + jnp.where(holds, ncol, 0) - jnp.where(self_held, 1, 0)
    pl.semaphore_wait(bar, greeted)

    @pl.when(holds)
    def _():
        each(
            ncol,
            lambda p: held_one(
                p, lambda: push(hs.at[p], tp0, s_h.at[0], tps.at[0], held_member(p))
            ),
            0,
        )

    push(v_ref, vg0.at[zh, y, x], s_one.at[0], z_sem.at[0], zpart)

    low, high = pl.ds(0, sub // 2), pl.ds(sub // 2, sub // 2)

    def gather_start(src, vg, unit, zd):
        if D_AG[unit]:
            to_plane(src, vg.at[zd, y, x], s_ag.at[unit, 0, 0], ag_sem.at[unit, 0, 0])
            return
        each(
            side,
            lambda k: push(
                src.at[low], vg.at[zd, y, x, low], s_ag.at[unit, 0, 0], ag_sem.at[unit, 0, 0], along(1, k)
            ),
        )
        each(
            side,
            lambda k: push(
                src.at[high], vg.at[zd, y, x, high], s_ag.at[unit, 1, 0], ag_sem.at[unit, 1, 0], along(0, k)
            ),
        )

    def gather_turn(vg, unit, zd):
        if D_AG[unit]:
            return
        take(vg.at[0, 0, pl.ds(0, side - 1), low], ag_sem.at[unit, 0, 0])
        part = vg.at[zd, y, :, low]
        each(side, lambda k: push(part, part, s_ag.at[unit, 0, 1], ag_sem.at[unit, 0, 1], along(0, k)))
        take(vg.at[0, 0, pl.ds(0, side - 1), low], ag_sem.at[unit, 1, 0])
        rest = vg.at[zd, :, x, high]
        each(side, lambda k: push(rest, rest, s_ag.at[unit, 1, 1], ag_sem.at[unit, 1, 1], along(1, k)))

    def gather_end(vg, unit):
        if D_AG[unit]:
            take(whole.at[0, 0, pl.ds(0, nxy - 1)], ag_sem.at[unit, 0, 0])
            return
        take(vg.at[0, pl.ds(0, side - 1), :, low], ag_sem.at[unit, 0, 1])
        take(vg.at[0, pl.ds(0, side - 1), :, low], ag_sem.at[unit, 1, 1])

    gather_start(v_ref, vg0, 0, zh)
    for b in range(band):

        @pl.when(row < b * ncol + col)
        def _(b=b):
            push(k_ref.at[b], ktr.at[home], s_one.at[4 + b], kq.at[home], mirror(b))

    def upright(pieces):
        return pieces[...].reshape(tile, 2 * sub).T[:sub]

    def paired(top):
        hi, lo = split(top)
        return jnp.concatenate(
            [jnp.concatenate([hi, hi], axis=1), jnp.concatenate([lo, jnp.zeros_like(lo)], axis=1)], axis=0
        )

    def spread_products(top, ps, it, turn):
        zd = other if turn == 0 else zh
        wide = jnp.dot(top, kk[zd, :, tile:], preferred_element_type=F32)
        wide = wide[:sub] + wide[sub:]
        for q in range(1, nxy):
            ps[zd, q // side, q % side] = wide[:, (q - 1) * tile : q * tile]
        if D_RS[it][turn]:

            def whole_one(k):
                at = lax.rem(xy + k, nxy)
                push(
                    ps.at[zd, at // side, lax.rem(at, side)],
                    whole.at[it, turn, xy],
                    s_rs.at[it, turn, 0, 0],
                    rs_sem.at[it, turn, 0, 0],
                    plane(k),
                )

            each(nxy, whole_one)
            return
        for half, (axis, rows) in enumerate(((0, low), (1, high))):

            def one(k, half=half, axis=axis, rows=rows):
                at = lax.rem((x if axis else y) + k, side)
                push(
                    ps.at[zd, :, at, rows] if axis else ps.at[zd, at, :, rows],
                    r1.at[it, turn, half, x if axis else y],
                    s_rs.at[it, turn, half, 0],
                    rs_sem.at[it, turn, half, 0],
                    along(axis, k),
                )

            each(side, one)

    def total_of(ref):
        total = ref[0]
        for n in range(1, side):
            total = total + ref[n]
        return total

    def sum_turn(ps, it, turn):
        if D_RS[it][turn]:
            return
        zd = other if turn == 0 else zh
        for half, (axis, rows) in enumerate(((0, low), (1, high))):
            take(r1.at[0, 0, 0, pl.ds(0, side - 1)], rs_sem.at[it, turn, half, 0])
            r1[it, turn, half, x if axis else y] = ps[zd, :, x, rows] if axis else ps[zd, y, :, rows]
            s2[it, turn, half] = total_of(r1.at[it, turn, half])
            here = y if axis else x
            r2[it, turn, half, here] = s2[it, turn, half, here]

            def one(k, half=half, axis=axis, here=here):
                push(
                    s2.at[it, turn, half, lax.rem(here + k, side)],
                    r2.at[it, turn, half, here],
                    s_rs.at[it, turn, half, 1],
                    rs_sem.at[it, turn, half, 1],
                    along(1 - axis, k),
                )

            each(side, one)

    def sum_end(ps, it, turn):
        if D_RS[it][turn]:
            take(whole.at[0, 0, pl.ds(0, nxy - 1)], rs_sem.at[it, turn, 0, 0])
            whole[it, turn, xy] = ps[other if turn == 0 else zh, y, x]
            total = whole[it, turn, 0]
            for n in range(1, nxy):
                total = total + whole[it, turn, n]
            return total
        halves = []
        for half in range(2):
            take(r2.at[0, 0, 0, pl.ds(0, side - 1)], rs_sem.at[it, turn, half, 1])
            halves.append(total_of(r2.at[it, turn, half]))
        return jnp.concatenate(halves, axis=0)

    def lay(vg, zd, first):
        for q in range(first, nxy):
            hi, lo = split(vg[zd, q // side, q % side])
            vc[zd, :sub, q * tile : (q + 1) * tile] = hi
            vc[zd, sub:, q * tile : (q + 1) * tile] = lo

    def direct(zd, first, last):
        cols = slice(first * tile, last * tile)
        both = nt(kk[zd, :, cols], vc[zd, :, cols])
        return both[:tile] + both[tile:]

    def scatter_direct(total, ds, dr, n):
        total = total + pltpu.roll(total, sub, 1)
        ds[...] = total.reshape(ds.shape)
        dr[col] = ds[col]

        def one(k):
            at = lax.rem(col + k, ncol)
            push(ds.at[at], dr.at[col], s_col.at[n], col_sem.at[n], in_col(k))

        each(ncol, one)

    def over_z(turn):
        zs[turn] = sum_end(ps1, 0, turn)
        push(zs.at[turn], zr.at[turn], s_one.at[1 + turn], z_sem.at[1 + turn], zpart)

    def line_sum(ref, count):
        total = ref[0]
        for p in range(1, count):
            total = total + ref[p]
        return total

    def piece_tile(piece):
        return jnp.concatenate([piece, jnp.zeros((tile - piece.shape[0], tile), F32)], axis=0).T[:sub]

    share = gs.shape[2]

    def gram_out(both, it):
        gram = nt_high(both, both)
        packed = jnp.concatenate([gram[: sub // 2], gram[sub // 2 :]], axis=1)
        for p in range(nxy):
            gs[it, p] = packed[p * share : (p + 1) * share]
        gr[it, xy] = gs[it, xy]

        def one(k):
            q = lax.rem(xy + k, nxy)
            push(gs.at[it, q], gr.at[it, xy], s_g.at[it, 0], g_sem.at[it, 0], plane(k))

        each(nxy, one)

    def gram_line(it):
        take(gr.at[it, pl.ds(0, nxy - 1)], g_sem.at[it, 0])
        gp[it] = line_sum(gr.at[it], nxy)
        gz[it, member] = gp[it]
        farthest_first(
            nline,
            lambda k: push(
                gp.at[it], gz.at[it, member], s_g.at[it, 1], g_sem.at[it, 1], in_line(k)
            ),
        )

    def gram_back(it):
        take(gz.at[it, pl.ds(0, nline - 1)], g_sem.at[it, 1])
        gq[it] = line_sum(gz.at[it], nline)
        ga[it, xy] = gq[it]
        to_plane(gq.at[it], ga.at[it, xy], s_g.at[it, 2], g_sem.at[it, 2])

    def gram_in(it):
        take(ga.at[it, pl.ds(0, nxy - 1)], g_sem.at[it, 2])
        packed = jnp.concatenate([ga[it, p] for p in range(nxy)], axis=0)
        return unpacked(packed) / order

    kept = {}

    def cut_kernel():
        for zd in range(2):
            ps1[zd, 0, 0] = jnp.zeros((sub, tile), F32)
            ps2[zd, 0, 0] = jnp.zeros((sub, tile), F32)
        for n in range(loads):
            load(n).wait()
            for at in range(max(n * chunk, 2), (n + 1) * chunk):
                q, zd = divmod(at, 2)
                hi, lo = split(kv[at])
                kk[zd, :tile, q * tile : (q + 1) * tile] = hi
                kk[zd, tile:, q * tile : (q + 1) * tile] = lo

    def own_turn():
        gather_turn(vg0, 0, zh)

    def other_start():
        take(vg0.at[other, y, x], z_sem.at[0])
        gather_start(vg0.at[other, y, x], vg0, 1, other)

    def other_turn():
        gather_turn(vg0, 1, other)

    def top_pieces():
        @pl.when(self_held)
        def _():
            tp0[...] = hs[col]

        @pl.when(jnp.logical_not(self_held))
        def _():
            take(tp0, tps.at[0])

        tg0[col] = tp0[...]
        each(ncol, lambda k: push(tp0, tg0.at[col], s_col.at[3], col_sem.at[3], in_col(k)))

    def mirrored():
        for b in range(band):

            @pl.when(row < b * ncol + col)
            def _(b=b):
                ktr[b] = kv[b]

            @pl.when(row == b * ncol + col)
            def _(b=b):
                ktr[b] = 0.5 * (kv[b] + kv[b].T)

            @pl.when(row > b * ncol + col)
            def _(b=b):
                take(ktr.at[b], kq.at[b])
                ktr[b] = ktr[b].T

            hi, lo = split(ktr[b])
            kk[b, :tile, :tile] = hi
            kk[b, tile:, :tile] = lo

    def direct_own():
        gather_end(vg0, 0)
        lay(vg0, zh, 0)
        kept["direct"] = direct(zh, 0, nxy)

    def direct_other():
        gather_end(vg0, 1)
        lay(vg0, other, 0)
        scatter_direct(kept["direct"] + direct(other, 0, nxy), ds1, dr1, 0)

    def spread_other():
        take(tg0.at[pl.ds(0, ncol - 1)], col_sem.at[3])
        kept["top"] = paired(upright(tg0))
        spread_products(kept["top"], ps1, 0, 0)

    def spread_own():
        spread_products(kept["top"], ps1, 0, 1)

    def turn_other():
        sum_turn(ps1, 0, 0)

    def turn_own():
        sum_turn(ps1, 0, 1)

    def z_other():
        over_z(0)

    def z_own():
        over_z(1)

    def direct_sum():
        take(dr1.at[pl.ds(0, ncol - 1)], col_sem.at[0])
        kept["piece"] = line_sum(dr1, ncol)
        tg1[col] = kept["piece"]
        each(ncol, lambda k: push(tg1.at[col], tg1.at[col], s_col.at[1], col_sem.at[1], in_col(k)))

    def top_tile():
        take(tg1.at[pl.ds(0, ncol - 1)], col_sem.at[1])
        top = upright(tg1)
        kept["top1"] = paired(top)

        @pl.when(is_root)
        def _():
            mine[0] = top
            push(mine.at[0], vtop.at[home], s_top.at[1], top_sem.at[home], zpart)
            to_plane(mine.at[0], vtop.at[home], s_top.at[0], top_sem.at[home])
            vtop[home] = top

    def spread_other1():
        spread_products(kept["top1"], ps2, 1, 0)

    def spread_own1():
        spread_products(kept["top1"], ps2, 1, 1)

    def own_tile():
        take(zr.at[0], z_sem.at[1])
        mine[1] = zs[1] + zr[0]
        vg1[zh, y, x] = mine[1]

    def gram_start():
        gram_out(jnp.concatenate([mine[1], piece_tile(kept["piece"])], axis=1), 0)

    def own_start1():
        gather_start(mine.at[1], vg1, 2, zh)

    def other_start1():
        take(zr.at[1], z_sem.at[2])
        mine[2] = zs[0] + zr[1]
        vg1[other, y, x] = mine[2]
        gather_start(mine.at[2], vg1, 3, other)

    def turn_other1():
        sum_turn(ps2, 1, 0)

    def turn_own1():
        sum_turn(ps2, 1, 1)

    def own_turn1():
        gather_turn(vg1, 2, zh)

    def other_turn1():
        gather_turn(vg1, 3, other)

    def gram_line0():
        gram_line(0)

    def gram_back0():
        gram_back(0)

    def z_other1():
        zs[2] = sum_end(ps2, 1, 0)
        push(zs.at[2], zr.at[2], s_one.at[3], z_sem.at[3], zpart)

    root_part = col == lax.rem(row + 1 - 2 * zh, ncol)

    def top_forward():
        @pl.when(root_part)
        def _():
            take(vtop.at[home], top_sem.at[home])
            to_plane(vtop.at[home], vtop.at[home], s_top.at[0], top_sem.at[home])

    def direct_own1():
        gather_end(vg1, 2)
        lay(vg1, zh, 1)
        kept["own1"] = direct(zh, 1, nxy)

    def direct_other1():
        gather_end(vg1, 3)
        lay(vg1, other, 1)
        kept["other1"] = direct(other, 1, nxy)

    def direct_top1():
        total = kept["own1"] + kept["other1"]
        for b in range(band):
            own = jnp.logical_and(home == b, jnp.logical_or(is_root, root_part))
            pl.when(jnp.logical_not(own))(
                functools.partial(lambda b: take(vtop.at[b], top_sem.at[b]), b)
            )
            hi, lo = split(vtop[b])
            vc[b, :sub, :tile] = hi
            vc[b, sub:, :tile] = lo
            total = total + direct(b, 0, 1)
        scatter_direct(total, ds2, dr2, 2)

    def rest_own1():
        kept["rest"] = sum_end(ps2, 1, 1)

    def factor0():
        kept["back"] = factorize(gram_in(0))[:, sub:]

    def direct_sum1():
        take(dr2.at[pl.ds(0, ncol - 1)], col_sem.at[2])
        hp[...] = line_sum(dr2, ncol)

        @pl.when(self_held)
        def _():
            hz[col] = hp[...]

        @pl.when(jnp.logical_not(self_held))
        def _():
            push(hp, hz.at[col], s_h.at[1], hz_sem.at[0], holder())

    steps = dict(
        cut_kernel=cut_kernel, own_turn=own_turn, other_start=other_start, other_turn=other_turn,
        top_pieces=top_pieces, mirrored=mirrored, direct_own=direct_own, direct_other=direct_other,
        spread_other=spread_other, spread_own=spread_own, turn_other=turn_other, turn_own=turn_own,
        z_other=z_other, z_own=z_own, direct_sum=direct_sum, top_tile=top_tile,
        spread_other1=spread_other1, spread_own1=spread_own1, own_tile=own_tile, gram_start=gram_start,
        own_start1=own_start1, other_start1=other_start1, turn_other1=turn_other1, turn_own1=turn_own1,
        own_turn1=own_turn1, other_turn1=other_turn1, gram_line0=gram_line0, gram_back0=gram_back0,
        z_other1=z_other1, top_forward=top_forward, direct_own1=direct_own1, direct_other1=direct_other1,
        direct_top1=direct_top1, rest_own1=rest_own1, factor0=factor0, direct_sum1=direct_sum1,
    )
    for name in ORDER:
        steps[name]()

    back = kept["back"]
    take(zr.at[2], z_sem.at[3])
    both = jnp.concatenate([kept["rest"] + zr[2], piece_tile(hp[...])], axis=1)
    both = jnp.dot(back, both, precision=HI, preferred_element_type=F32)
    gram_out(both, 1)
    mine[3] = both[:, :tile]
    gram_line(1)

    @pl.when(holds)
    def _():
        pl.when(self_held)(lambda: take(hz.at[pl.ds(0, ncol - 1)], hz_sem.at[0]))
        pl.when(jnp.logical_not(self_held))(lambda: take(hz, hz_sem.at[0]))
        mine[3] = jnp.dot(back, upright(hz), precision=HI, preferred_element_type=F32)

    gram_back(1)
    take(ga.at[1, pl.ds(0, nxy - 1)], g_sem.at[1, 2])
    gram_ref[...] = jnp.concatenate([ga[1, p] for p in range(nxy)], axis=0)
    last_ref[...] = mine[3]

    many = nxy - 1
    take(mine.at[0], s_one.at[0])
    for n in range(3):
        take(zs.at[n], s_one.at[1 + n])
    for b in range(band):
        pl.when(row < b * ncol + col)(
            functools.partial(lambda b: take(kv.at[b], s_one.at[4 + b]), b)
        )
    for unit in range(4):
        if D_AG[unit]:
            take(whole.at[0, 0, pl.ds(0, many)], s_ag.at[unit, 0, 0])
            continue
        for half in range(2):
            take(vg0.at[0, 0, pl.ds(0, side - 1), low], s_ag.at[unit, half, 0])
            take(vg0.at[0, pl.ds(0, side - 1), :, low], s_ag.at[unit, half, 1])

    @pl.when(holds)
    def _():
        pl.when(self_held)(lambda: take(hs.at[pl.ds(0, ncol - 1)], s_h.at[0]))
        pl.when(jnp.logical_not(self_held))(lambda: take(hs, s_h.at[0]))

    pl.when(jnp.logical_not(self_held))(lambda: take(hp, s_h.at[1]))
    for n in range(4):
        take(tg1.at[pl.ds(0, ncol - 1)], s_col.at[n])
    for it in range(2):
        for turn in range(2):
            if D_RS[it][turn]:
                take(whole.at[0, 0, pl.ds(0, many)], s_rs.at[it, turn, 0, 0])
                continue
            for half in range(2):
                take(r1.at[0, 0, 0, pl.ds(0, side - 1)], s_rs.at[it, turn, half, 0])
                take(r2.at[0, 0, 0, pl.ds(0, side - 1)], s_rs.at[it, turn, half, 1])
        take(gs.at[it, pl.ds(0, many)], s_g.at[it, 0])
        take(gz.at[it, pl.ds(0, nline - 1)], s_g.at[it, 1])
        take(gs.at[it, pl.ds(0, many)], s_g.at[it, 2])

    @pl.when(is_root)
    def _():
        take(mine.at[0], s_top.at[1])

    @pl.when(jnp.logical_or(is_root, root_part))
    def _():
        take(whole.at[0, 0, pl.ds(0, many)], s_top.at[0])


def per_device(nrow, ncol, kernel_tiles, basis):
    tiles, tile = kernel_tiles.shape[2], kernel_tiles.shape[3]
    sub = basis.shape[0]
    nxy, band, nline = nrow // 2, nrow // ncol, 2 * ncol
    pieces = (ncol, tile // ncol, 2 * sub)
    share = sub // 2 // nxy
    wide = 2 * sub
    vmem = lambda shape, kind=F32: pltpu.VMEM(shape, kind)
    dma = lambda *shape: pltpu.SemaphoreType.DMA(shape)
    side = 4 if nxy == 16 else 2
    halves = (2, 2, 2, side)
    half = (sub // 2, tile)
    planes = (2, side, nxy // side, sub, tile)
    scratch = [
        vmem((tiles, tile, tile)),
        vmem((2, 2 * tile, nxy * tile), BF16),
        vmem((2, 2 * sub, nxy * tile), BF16), vmem((band, tile, tile)),
        vmem(planes), vmem(planes), vmem((band, sub, tile)), vmem(planes), vmem(planes),
        vmem((2, 2, nxy, sub, tile)),
        vmem(halves + (side,) + half), vmem(halves + half), vmem(halves + half),
        vmem((3, sub, tile)), vmem((3, sub, tile)), vmem((4, sub, tile)),
        vmem(pieces), vmem(pieces), vmem(pieces), vmem(pieces),
        vmem(pieces), vmem(pieces[1:]), vmem(pieces), vmem(pieces), vmem(pieces[1:]), vmem(pieces),
        vmem((2, nxy, share, wide)), vmem((2, nxy, share, wide)), vmem((2, share, wide)),
        vmem((2, nline, share, wide)), vmem((2, share, wide)), vmem((2, nxy, share, wide)),
        dma(5), dma(band), dma(1), dma(4), dma(4, 2, 2), dma(2, 2, 2, 2), dma(4), dma(band), dma(1),
        dma(2, 3),
        dma(4 + band), dma(4, 2, 2), dma(2, 2, 2, 2), dma(4), dma(2), dma(2, 3), dma(2),
    ]
    flops = 2 * 3 * 4 * tiles * tile * tile * sub
    gram, last = pl.pallas_call(
        functools.partial(kernel, nrow, ncol),
        out_shape=(
            jax.ShapeDtypeStruct((sub // 2, 2 * sub), F32),
            jax.ShapeDtypeStruct((sub, tile), F32),
        ),
        in_specs=[pl.BlockSpec(memory_space=pltpu.HBM)] * 2,
        out_specs=(pl.BlockSpec(memory_space=pltpu.VMEM),) * 2,
        scratch_shapes=scratch,
        compiler_params=pltpu.CompilerParams(
            collective_id=0, has_side_effects=True, vmem_limit_bytes=63 * 1024 * 1024
        ),
        cost_estimate=pl.CostEstimate(
            flops=flops, bytes_accessed=4 * tiles * tile * tile, transcendentals=0
        ),
        name="subspace",
    )(kernel_tiles[0, 0], basis.reshape(sub, tile))
    out, chol = pl.pallas_call(
        functools.partial(finish, nrow * ncol * tile),
        out_shape=(
            jax.ShapeDtypeStruct((sub, tile), F32),
            jax.ShapeDtypeStruct((sub, sub), F32),
        ),
        in_specs=[pl.BlockSpec(memory_space=pltpu.VMEM)] * 2,
        out_specs=(pl.BlockSpec(memory_space=pltpu.VMEM),) * 2,
        name="finish",
    )(gram, last)
    return out.reshape(sub, 1, 1, tile), chol


def solution(mesh):
    nrow, ncol = mesh.shape["row"], mesh.shape["col"]
    return jax.shard_map(
        functools.partial(per_device, nrow, ncol),
        mesh=mesh,
        in_specs=(P("row", "col", None, None, None), P(None, "row", "col", None)),
        out_specs=(P(None, "row", "col", None), P()),
        check_vma=False,
    )
```
